128 devices in a mesh: row: 8 (over x_lo, z), col: 16 (over y, x_hi, core).
Axes of the slice: x: 4 (x_hi: 2, x_lo: 2; x = x_hi * 2 + x_lo), y: 4, z: 4, core: 2. Of those that a mesh axis runs over, the one named last changes fastest.
Arguments:
- pool: bfloat16 [24576, 128], P(('row', 'col')), may hold values from -20 to 20
- labeled: bfloat16 [24576, 128], P(('row', 'col')), may hold values from -20 to 20
Outputs:
- grad_pool: float32 [24576, 128], P(('row', 'col'))
- grad_label: float32 [24576, 128], P(('row', 'col'))
- objective: float32 [], replicated
The draws below stay inside these ranges and needn't reach their ends.
All inputs are finite; a program needn't handle non-finite values.
Results may differ from the reference program's by a relative error of at most 0.03.
Values may be sent and summed in bfloat16 or wider, within the bound.
A program may use at most 64 MiB of HBM per device.

```python
import jax
import jax.numpy as jnp
from jax import lax

EMB = 128
OWN = 192
POINTS = 24576
N_ROW = 8
N_COL = 16


def latent_map(key):
    return jax.random.normal(key, (6, EMB), jnp.float32) * 1.2


def embedding(latent, noise_part, projection):
    values = noise_part * 0.7
    for latent_dim in range(6):
        values = values + latent[:, latent_dim:latent_dim + 1] * projection[latent_dim][None, :]
    return jnp.clip(values, -20.0, 20.0).astype(jnp.bfloat16)


def owner_shift(step_size):
    owner = jnp.arange(POINTS, dtype=jnp.int32) // OWN
    row_place = (owner // N_COL).astype(jnp.float32) / float(max(N_ROW - 1, 1))
    col_place = (owner % N_COL).astype(jnp.float32) / float(max(N_COL - 1, 1))
    return 1.1 + step_size * (row_place + col_place)


def draw_pool(key, part):
    projection = latent_map(key)
    key = jax.random.fold_in(key, 5)
    latent_key, noise_key, scale_key = jax.random.split(key, 3)
    latent = jnp.clip(jax.random.normal(latent_key, (POINTS, 6), jnp.float32), -6.0, 6.0)
    noise_part = jnp.clip(jax.random.normal(noise_key, (POINTS, EMB), jnp.float32), -6.0, 6.0)
    shift = owner_shift(0.9)
    jitter = jax.random.uniform(scale_key, (POINTS,), jnp.float32, 0.9, 1.1)
    offset = jnp.where(jnp.arange(6) == 0, 1.0, 0.0).astype(jnp.float32)
    return embedding(latent * jitter[:, None] + shift[:, None] * offset[None, :], noise_part, projection)


def draw_labeled(key, part):
    projection = latent_map(key)
    key = jax.random.fold_in(key, 7)
    latent_key, noise_key, scale_key = jax.random.split(key, 3)
    latent = jnp.clip(jax.random.normal(latent_key, (POINTS, 6), jnp.float32), -6.0, 6.0)
    noise_part = jnp.clip(jax.random.normal(noise_key, (POINTS, EMB), jnp.float32), -6.0, 6.0)
    position = jnp.arange(POINTS, dtype=jnp.float32) / POINTS
    jitter = jax.random.uniform(scale_key, (POINTS,), jnp.float32, 0.9, 1.1)
    spread = 0.75 * jnp.exp(0.55 * position) * jitter
    offset = jnp.where(jnp.arange(6) == 0, 0.5, 0.0).astype(jnp.float32)
    return embedding(latent * spread[:, None] + offset[None, :], noise_part, projection)


def setup_inputs(seed: int = 0) -> dict:
    key_list = jax.random.split(jax.random.key(seed), 3)
    pool = draw_pool(jax.random.fold_in(key_list[2], 71), 0)
    labeled = draw_labeled(jax.random.fold_in(key_list[2], 71), 0)
    return dict(pool=pool, labeled=labeled)


def squared_norms(values):
    return lax.optimization_barrier(jnp.sum(jnp.square(values.astype(jnp.float32)), axis=1))

def gram_kernel(left_rows, left_norms, right_rows, right_norms):
    products = lax.dot_general(left_rows, right_rows, (((1,), (1,)), ((), ())), preferred_element_type=jnp.float32)
    distance = left_norms[:, None] + right_norms[None, :] - 2.0 * products
    return jnp.exp(distance * (-0.5 / left_rows.shape[1]))

def reference(pool, labeled):
    count = POINTS
    block_rows = 512 if count % 512 == 0 else count
    block_count = count // block_rows
    pool_norms = squared_norms(pool)
    label_norms = squared_norms(labeled)
    pool_blocks = pool.reshape(block_count, block_rows, EMB)
    label_blocks = labeled.reshape(block_count, block_rows, EMB)
    pool_nblocks = pool_norms.reshape(block_count, block_rows)
    label_nblocks = label_norms.reshape(block_count, block_rows)

    def first_pass(column_sums, pieces):
        pool_part, label_part, pool_npart, label_npart = pieces
        kernel_xx = gram_kernel(pool_part, pool_npart, pool, pool_norms)
        kernel_yy = gram_kernel(label_part, label_npart, labeled, label_norms)
        kernel_xy = gram_kernel(pool_part, pool_npart, labeled, label_norms)
        row_part = lax.optimization_barrier(jnp.sum(kernel_xx + kernel_yy - kernel_xy, axis=1))
        return (column_sums + lax.optimization_barrier(jnp.sum(kernel_xy, axis=0)), row_part)
    column_sums, row_parts = lax.scan(first_pass, jnp.zeros((count,), jnp.float32), (pool_blocks, label_blocks, pool_nblocks, label_nblocks))
    row_totals = row_parts.reshape(count) - column_sums
    mean_row = jnp.sum(row_totals) / count
    statistic = mean_row / count
    centred = row_totals - mean_row
    variance = 4.0 * jnp.sum(jnp.square(centred)) / float(count) ** 3 + 1e-08
    objective = statistic / jnp.sqrt(variance)
    coef_a = 1.0 / (count * jnp.sqrt(variance))
    coef_b = -4.0 * statistic / (float(count) ** 2 * variance ** 1.5)
    centred_blocks = centred.reshape(block_count, block_rows)

    def second_pass(label_column, pieces):
        pool_part, label_part, pool_npart, label_npart, centre_part = pieces
        pair_weight = 2.0 * coef_a + coef_b * (centre_part[:, None] + centred[None, :])
        weight_xx = pair_weight * gram_kernel(pool_part, pool_npart, pool, pool_norms)
        weight_yy = pair_weight * gram_kernel(label_part, label_npart, labeled, label_norms)
        weight_xy = pair_weight * gram_kernel(pool_part, pool_npart, labeled, label_norms)
        xy_rounded = weight_xy.astype(jnp.bfloat16)
        pool_grad = pool_part.astype(jnp.float32) * lax.optimization_barrier(jnp.sum(weight_xx - weight_xy, axis=1))[:, None]
        pool_grad = pool_grad - jnp.dot(weight_xx.astype(jnp.bfloat16), pool, preferred_element_type=jnp.float32)
        pool_grad = pool_grad + jnp.dot(xy_rounded, labeled, preferred_element_type=jnp.float32)
        label_grad = label_part.astype(jnp.float32) * lax.optimization_barrier(jnp.sum(weight_yy, axis=1))[:, None]
        label_grad = label_grad - jnp.dot(weight_yy.astype(jnp.bfloat16), labeled, preferred_element_type=jnp.float32)
        cross = labeled.astype(jnp.float32) * lax.optimization_barrier(jnp.sum(weight_xy, axis=0))[:, None]
        cross = cross - lax.dot_general(xy_rounded, pool_part, (((0,), (0,)), ((), ())), preferred_element_type=jnp.float32)
        return (label_column + cross, (pool_grad, label_grad))
    label_column, grads = lax.scan(second_pass, jnp.zeros((count, EMB), jnp.float32), (pool_blocks, label_blocks, pool_nblocks, label_nblocks, centred_blocks))
    grad_pool = -grads[0].reshape(count, EMB) / EMB
    grad_label = (label_column - grads[1].reshape(count, EMB)) / EMB
    return (grad_pool, grad_label, objective)
```

```python
import math

import jax
import jax.numpy as jnp
from jax import lax
from jax.experimental import pallas as pl
from jax.experimental.pallas import tpu as pltpu
from jax.sharding import PartitionSpec as P

MESH = pl.DeviceIdType.MESH
F32 = jnp.float32
BF16 = jnp.bfloat16

FIRST = tuple((dx, dk) for dx in range(4) for dk in range(2))
SECOND = ((0, 1), (1, 0), (-1, -1), (-1, 1), (1, 2), (2, -1), (0, 0), (0, 2), (2, 0), (2, 2))
OWN_FIRST = FIRST.index((0, 0))
OWN_SECOND = SECOND.index((0, 0))
TWO_SIDED = 3
SECOND_PAIRS = len(SECOND) // 2


def place():
    row, col = lax.axis_index("row"), lax.axis_index("col")
    return ((col // 2) % 2) * 2 + row // 4, col // 4, row % 4, col % 2


def device(x, y, z, core):
    x, y, z, core = (x + 8) % 4, (y + 8) % 4, (z + 8) % 4, (core + 2) % 2
    return ((x % 2) * 4 + z, y * 4 + (x // 2) * 2 + core)


def split3(value):
    high = value.astype(BF16).astype(F32)
    rest = value - high
    middle = rest.astype(BF16).astype(F32)
    return high, middle, rest - middle


def matmul(left, right):
    return lax.dot_general(left, right, (((1,), (0,)), ((), ())), preferred_element_type=F32)


def matmul_t(left, right):
    return lax.dot_general(left, right, (((1,), (1,)), ((), ())), preferred_element_type=F32)


def kernel(
    pool_ref, label_ref, grad_pool_ref, grad_label_ref, objective_ref,
    own, at, bt, za, km, acc_a, acc_b, part_a, part_b, part_in, t_own, ta, tb,
    w1a, w1b, w2a, w2b, o1a, o1b, o2a, o2b, ga, gb, g_in, stat_out, stat_in,
    ga_send, ga_recv, gb_send, gb_recv, pa_send, pa_recv, pb_send, pb_recv,
    ta_send, ta_recv, tb_send, tb_recv, ra_send, ra_recv, rb_send, rb_recv, st_send, st_recv,
):
    width = pool_ref.shape[1]
    each = pool_ref.shape[0]
    both = 2 * each
    deep = width + 16
    na, nb = len(FIRST), len(SECOND)
    points = float(each * 128)
    x, y, z, core = place()

    def to_first(a):
        dx, dk = FIRST[a]
        return device(x + dx, y, z, core + dk)

    def from_first(a):
        dx, dk = FIRST[a]
        return device(x - dx, y, z, core + dk)

    def to_second(b):
        dy, dz = SECOND[b]
        return device(x, y + dy, z + dz, core)

    def from_second(b):
        dy, dz = SECOND[b]
        return device(x, y - dy, z - dz, core)

    def copy(src, dst, send, recv, target):
        return pltpu.make_async_remote_copy(
            src_ref=src, dst_ref=dst, send_sem=send, recv_sem=recv, device_id=target, device_id_type=MESH
        )

    first_others = [a for a in range(na) if a != OWN_FIRST]
    second_others = [b for b in range(nb) if b != OWN_SECOND]

    def lanes(index, count=1):
        return pl.ds(pl.multiple_of(index * both * count, both * count), both * count)

    partners = set()
    for a in first_others:
        dx, dk = FIRST[a]
        partners.add((dx, 0, 0, dk))
    for b in second_others:
        dy, dz = SECOND[b]
        partners.add((0, dy % 4, dz % 4, 0))
        partners.add((0, -dy % 4, -dz % 4, 0))
    barrier = pltpu.get_barrier_semaphore()
    for dx, dy, dz, dk in sorted(partners):
        pl.semaphore_signal(
            barrier, inc=1, device_id=device(x + dx, y + dy, z + dz, core + dk), device_id_type=MESH
        )

    sign = jnp.where(lax.broadcasted_iota(jnp.int32, (1, both), 1) < each, 1.0, -1.0).astype(F32)
    rows = jnp.concatenate([pool_ref[...].astype(F32), label_ref[...].astype(F32)], axis=0)
    cols = rows.T
    half = jnp.sum(cols * cols, axis=0, keepdims=True) * -0.5
    high, middle, low = split3(half)
    place16 = lax.broadcasted_iota(jnp.int32, (16, both), 0)
    tail = jnp.where(place16 == 0, high, jnp.where(place16 == 1, middle, jnp.where(place16 == 2, low, 0.0)))
    tail = jnp.where((place16 >= 8) & (place16 < 11), 1.0, tail)
    block = jnp.concatenate([cols, tail], axis=0).astype(BF16)
    own[...] = block
    at[:, pl.ds(OWN_FIRST * both, both)] = block
    bt[0:deep, pl.ds(OWN_SECOND * both, both)] = block
    bt[deep:, :] = jnp.zeros((bt.shape[0] - deep, nb * both), BF16)
    acc_a[...] = jnp.zeros(acc_a.shape, F32)
    acc_b[...] = jnp.zeros(acc_b.shape, F32)

    pl.semaphore_wait(barrier, len(partners))

    gathers = []
    for a in first_others[:1]:
        gathers.append(copy(own, at.at[:, pl.ds(a * both, both)], ga_send.at[a], ga_recv.at[a], from_first(a)))
    for b in second_others:
        gathers.append(
            copy(own, bt.at[pl.ds(0, deep), pl.ds(b * both, both)], gb_send.at[b], gb_recv.at[b], from_second(b))
        )
    for a in first_others[1:]:
        gathers.append(copy(own, at.at[:, pl.ds(a * both, both)], ga_send.at[a], ga_recv.at[a], from_first(a)))
    for item in gathers:
        item.start()

    one_row = jnp.where(lax.broadcasted_iota(jnp.int32, (16, both), 0) == 0, sign, 0.0)

    def take_first(a):
        here = lanes(a)
        value = at[:, here].astype(F32)
        za[here, 0:width] = value[0:width].T.astype(BF16)
        rest = jnp.concatenate(
            [value[width + 8 : width + 16], value[width : width + 8], jnp.zeros((width - 16, both), F32)], axis=0
        )
        za[here, width : 2 * width] = rest.T.astype(BF16)
        w1a[0:width, here] = (value[0:width] * sign).astype(BF16)
        w1a[width:deep, here] = one_row.astype(BF16)

    def take_second(b):
        here = lanes(b)
        value = bt[0:width, here].astype(F32)
        w1b[0:width, here] = (value * sign).astype(BF16)
        w1b[width:deep, here] = one_row.astype(BF16)

    scale = math.log2(math.e) / width
    tile_sign = sign[:, 128:256]

    def second_step(i, carry):
        pair = i + jnp.where(i == 2, 1, 0) - jnp.where(i == 3, 1, 0)

        def await_second(b):
            @pl.when(b != OWN_SECOND)
            def _():
                copy(
                    own, bt.at[pl.ds(0, deep), lanes(b)], gb_send.at[b], gb_recv.at[b], device(x, y, z, core)
                ).wait_recv()

            take_second(b)

        await_second(2 * pair)
        await_second(2 * pair + 1)
        wide = lanes(pair, 2)

        def first_step(a, carry):
            here = lanes(a)

            @pl.when((i == 0) & (a != OWN_FIRST))
            def _():
                copy(own, at.at[:, here], ga_send.at[a], ga_recv.at[a], device(x, y, z, core)).wait_recv()

            @pl.when(i == 0)
            def _():
                take_first(a)

            product = matmul(za[here, :], bt[:, wide])
            value = jnp.exp2(product * scale)
            km[here, wide] = value.astype(BF16)
            tiles = [value[:, 128 * j : 128 * (j + 1)] for j in range(6)]
            across = (tiles[0] - tiles[2]) + (tiles[3] - tiles[5]) + (tiles[1] + tiles[4]) * tile_sign
            acc_a[here, :] += across
            down = jnp.sum(value[0:each].reshape(each // 8, 8, 2 * both), axis=0)
            down = down - jnp.sum(value[each:both].reshape(each // 8, 8, 2 * both), axis=0)
            unused = (pair >= TWO_SIDED) & ((a < 2) | (a >= 4))
            to = pl.multiple_of(jnp.where(unused, 8, 0), 8)
            acc_b[pl.ds(to, 8), wide] += down
            return carry

        lax.fori_loop(0, jnp.where(pair < TWO_SIDED, na, 6), first_step, 0)
        return carry

    lax.fori_loop(0, SECOND_PAIRS, second_step, 0)

    for b in range(nb):
        here = pl.ds(b * both, both)
        part_b[:, here] = jnp.broadcast_to(jnp.sum(acc_b[0:8, here], axis=0, keepdims=True) * sign, (8, both))
    partials = []
    for b in second_others:
        here = pl.ds(b * both, both)
        partials.append(copy(part_b.at[:, here], part_in.at[na + b], pb_send.at[b], pb_recv.at[b], to_second(b)))
        partials[-1].start()
    for a in list(reversed(first_others)) + [OWN_FIRST]:
        here = pl.ds(a * both, both)
        total = jnp.sum(acc_a[here, :].T, axis=0, keepdims=True) * sign
        part_a[:, here] = jnp.broadcast_to(total, (8, both))
        if a != OWN_FIRST:
            partials.append(copy(part_a.at[:, here], part_in.at[a], pa_send.at[a], pa_recv.at[a], to_first(a)))
            partials[-1].start()

    inner = TWO_SIDED * 2 * both

    def sum_first(w, out, w_cols, ap):
        here = lanes(ap, 2)
        out[:, here] = matmul_t(w[:, 0:w_cols], km[here, 0:w_cols])

    def sum_second(w, out, bp, lo, hi):
        here = lanes(bp, 2)
        out[:, here] = matmul(w[:, lo:hi], km[lo:hi, here])

    def all_sums(wa, wb, oa, ob):
        def body_b(bp, carry):
            sum_second(wa, ob, bp, 0, na * both)
            return carry

        def body_b2(bp, carry):
            sum_second(wa, ob, bp, 2 * both, 4 * both)
            return carry

        def body_a(ap, carry):
            sum_first(wb, oa, nb * both, ap)
            return carry

        lax.fori_loop(0, TWO_SIDED, body_b, 0)
        lax.fori_loop(TWO_SIDED, SECOND_PAIRS, body_b2, 0)
        lax.fori_loop(0, 3, body_a, 0)
        sum_first(wb, oa, inner, 3)

    all_sums(w1a, w1b, o1a, o1b)

    for item in partials:
        item.wait_recv()
    total = part_a[:, pl.ds(OWN_FIRST * both, both)] + part_b[:, pl.ds(OWN_SECOND * both, both)]
    for a in first_others:
        total = total + part_in[a]
    for b in second_others:
        total = total + part_in[na + b]
    total = total + pltpu.roll(total, each, 1)
    t_own[...] = total
    ta[:, pl.ds(OWN_FIRST * both, both)] = total
    tb[:, pl.ds(OWN_SECOND * both, both)] = total
    totals = []
    for a in first_others:
        totals.append(copy(t_own, ta.at[:, pl.ds(a * both, both)], ta_send.at[a], ta_recv.at[a], from_first(a)))
    for b in second_others:
        totals.append(copy(t_own, tb.at[:, pl.ds(b * both, both)], tb_send.at[b], tb_recv.at[b], from_second(b)))
    for item in totals:
        item.start()
    for item in totals[: len(first_others)]:
        item.wait_recv()

    line = ta[0:1, :]
    mean = jnp.sum(line, axis=1, keepdims=True) / (na * both)
    spread = 0.5 * jnp.sum(jnp.square(line - mean), axis=1, keepdims=True)

    def send_stats(stage, mean, spread):
        half_lane = lax.broadcasted_iota(jnp.int32, (8, 128), 1) < 64
        stat_out[stage] = jnp.where(half_lane, mean, spread)
        items = []
        for step in range(1, 4):
            target = device(x, y - step, z, core) if stage == 0 else device(x, y, z - step, core)
            slot = stage * 3 + step - 1
            items.append(copy(stat_out.at[stage], stat_in.at[slot], st_send.at[slot], st_recv.at[slot], target))
            items[-1].start()
        return items

    def merge_stats(stage, items, mean, spread, count):
        means, spreads = [mean], [spread]
        for item in items:
            item.wait_recv()
        for step in range(3):
            value = stat_in[stage * 3 + step]
            means.append(value[0:1, 0:1])
            spreads.append(value[0:1, 64:65])
        middle = (means[0] + means[1] + means[2] + means[3]) * 0.25
        total = spreads[0] + spreads[1] + spreads[2] + spreads[3]
        for value in means:
            total = total + count * jnp.square(value - middle)
        return middle, total

    stats_y = send_stats(0, mean, spread)
    for item in totals[len(first_others) :]:
        item.wait_recv()

    local = (jnp.sum(ta[0:1, :], axis=1, keepdims=True) + jnp.sum(tb[0:1, :], axis=1, keepdims=True)) / (
        (na + nb) * both
    )

    def weigh(t_ref, w1, w2, index):
        here = lanes(index)
        shifted = t_ref[0:1, here] - local
        w2[0:width, here] = (w1[0:width, here].astype(F32) * shifted).astype(BF16)
        high, middle, low = split3(shifted * sign)
        rows3 = jnp.where(place16 == 0, high, jnp.where(place16 == 1, middle, jnp.where(place16 == 2, low, 0.0)))
        w2[width:deep, here] = rows3.astype(BF16)

    def weigh_first(a, carry):
        weigh(ta, w1a, w2a, a)
        return carry

    def weigh_second(b, carry):
        weigh(tb, w1b, w2b, b)
        return carry

    lax.fori_loop(0, na, weigh_first, 0)
    lax.fori_loop(0, nb, weigh_second, 0)
    count8 = float(na * each)
    mean, spread = merge_stats(0, stats_y, mean, spread, count8)
    stats_z = send_stats(1, mean, spread)
    all_sums(w2a, w2b, o2a, o2b)
    mean, spread = merge_stats(1, stats_z, mean, spread, 4.0 * count8)

    variance = 4.0 * spread / points**3 + 1e-08
    statistic = mean / points
    deviation = jnp.sqrt(variance)
    coef_a = 1.0 / (points * deviation)
    coef_b = -4.0 * statistic / (points**2 * (variance * deviation))
    objective_ref[...] = jnp.broadcast_to(statistic / deviation, objective_ref.shape)
    base = 2.0 * coef_a + 2.0 * coef_b * (local - mean)

    def gradient(rows_ref, t_ref, o1, o2, index):
        here = pl.ds(index * both, both)
        value = rows_ref[0:width, here].astype(F32)
        plain = value * o1[width : width + 1, here] - o1[0:width, here]
        rho = o2[width : width + 1, here] + o2[width + 1 : width + 2, here] + o2[width + 2 : width + 3, here]
        weighted = value * rho - o2[0:width, here]
        alpha = base + coef_b * (t_ref[0:1, here] - local)
        outer = sign * (-1.0 / width)
        return plain * (alpha * outer) + weighted * (coef_b * outer)

    returns = []
    for b in reversed(second_others):
        here = pl.ds(b * both, both)
        gb[:, here] = gradient(bt, tb, o1b, o2b, b).astype(BF16)
        returns.append(copy(gb.at[:, here], g_in.at[na + b], rb_send.at[b], rb_recv.at[b], to_second(b)))
        returns[-1].start()
    for a in reversed(first_others):
        here = pl.ds(a * both, both)
        ga[:, here] = gradient(at, ta, o1a, o2a, a).astype(BF16)
        returns.append(copy(ga.at[:, here], g_in.at[a], ra_send.at[a], ra_recv.at[a], to_first(a)))
        returns[-1].start()
    result = gradient(at, ta, o1a, o2a, OWN_FIRST) + gradient(bt, tb, o1b, o2b, OWN_SECOND)
    for item in returns:
        item.wait_recv()
    for a in first_others:
        result = result + g_in[a].astype(F32)
    for b in second_others:
        result = result + g_in[na + b].astype(F32)
    result = result.T
    grad_pool_ref[...] = result[0:each]
    grad_label_ref[...] = result[each:both]

    for item in gathers + partials + totals + stats_y + stats_z + returns:
        item.wait_send()


def shards(pool, labeled):
    each, width = pool.shape
    both = 2 * each
    deep = width + 16
    na, nb = len(FIRST), len(SECOND)
    la, lb = na * both, nb * both
    dma = pltpu.SemaphoreType.DMA
    vmem = pl.BlockSpec(memory_space=pltpu.VMEM)
    scratch = [
        pltpu.VMEM((deep, both), BF16),
        pltpu.VMEM((deep, la), BF16),
        pltpu.VMEM((2 * width, lb), BF16),
        pltpu.VMEM((la, 2 * width), BF16),
        pltpu.VMEM((la, lb), BF16),
        pltpu.VMEM((la, 128), F32),
        pltpu.VMEM((16, lb), F32),
        pltpu.VMEM((8, la), F32),
        pltpu.VMEM((8, lb), F32),
        pltpu.VMEM((na + nb, 8, both), F32),
        pltpu.VMEM((8, both), F32),
        pltpu.VMEM((8, la), F32),
        pltpu.VMEM((8, lb), F32),
        pltpu.VMEM((deep, la), BF16),
        pltpu.VMEM((deep, lb), BF16),
        pltpu.VMEM((deep, la), BF16),
        pltpu.VMEM((deep, lb), BF16),
        pltpu.VMEM((deep, la), F32),
        pltpu.VMEM((deep, lb), F32),
        pltpu.VMEM((deep, la), F32),
        pltpu.VMEM((deep, lb), F32),
        pltpu.VMEM((width, la), BF16),
        pltpu.VMEM((width, lb), BF16),
        pltpu.VMEM((na + nb, width, both), BF16),
        pltpu.VMEM((2, 8, 128), F32),
        pltpu.VMEM((6, 8, 128), F32),
    ]
    for _ in range(4):
        scratch += [dma((na,)), dma((na,)), dma((nb,)), dma((nb,))]
    scratch += [dma((6,)), dma((6,))]
    grad_pool, grad_label, objective = pl.pallas_call(
        kernel,
        out_shape=(
            jax.ShapeDtypeStruct((each, width), F32),
            jax.ShapeDtypeStruct((each, width), F32),
            jax.ShapeDtypeStruct((8, 128), F32),
        ),
        in_specs=[vmem, vmem],
        out_specs=(vmem, vmem, vmem),
        scratch_shapes=scratch,
        compiler_params=pltpu.CompilerParams(
            collective_id=0, has_side_effects=True, vmem_limit_bytes=60 * 2**20
        ),
    )(pool, labeled)
    return grad_pool, grad_label, objective[0, 0]


def solution(mesh):
    in_specs = (P(("row", "col"), None), P(("row", "col"), None))
    out_specs = (P(("row", "col"), None), P(("row", "col"), None), P())
    return jax.shard_map(shards, mesh=mesh, in_specs=in_specs, out_specs=out_specs, check_vma=False)
```

```python
import math

import jax
import jax.numpy as jnp
from jax import lax
from jax.experimental import pallas as pl
from jax.experimental.pallas import tpu as pltpu
from jax.sharding import PartitionSpec as P

MESH = pl.DeviceIdType.MESH
F32 = jnp.float32
BF16 = jnp.bfloat16

FIRST = tuple((dx, dk) for dx in range(4) for dk in range(2))
SECOND = ((0, 1), (1, 0), (-1, -1), (-1, 1), (1, 2), (2, -1), (0, 0), (0, 2), (2, 0), (2, 2))
OWN_FIRST = FIRST.index((0, 0))
OWN_SECOND = SECOND.index((0, 0))
TWO_SIDED = 3
SECOND_PAIRS = len(SECOND) // 2


def place():
    row, col = lax.axis_index("row"), lax.axis_index("col")
    return ((col // 2) % 2) * 2 + row // 4, col // 4, row % 4, col % 2


def device(x, y, z, core):
    x, y, z, core = (x + 8) % 4, (y + 8) % 4, (z + 8) % 4, (core + 2) % 2
    return ((x % 2) * 4 + z, y * 4 + (x // 2) * 2 + core)


def split3(value):
    high = value.astype(BF16).astype(F32)
    rest = value - high
    middle = rest.astype(BF16).astype(F32)
    return high, middle, rest - middle


def matmul(left, right):
    return lax.dot_general(left, right, (((1,), (0,)), ((), ())), preferred_element_type=F32)


def matmul_t(left, right):
    return lax.dot_general(left, right, (((1,), (1,)), ((), ())), preferred_element_type=F32)


def pick(index, values):
    out = values[-1]
    for i in range(len(values) - 2, -1, -1):
        out = jnp.where(index == i, values[i], out)
    return out


def kernel(
    pool_ref, label_ref, grad_pool_ref, grad_label_ref, objective_ref,
    own, at, bt, za, km, acc_a, acc_b, part_a, part_b, part_in, t_own, ta, tb,
    w1a, w2a, wb, o1b, o2b, oa, ga, gb, g_in, stat_out, stat_in,
    ga_send, ga_recv, gb_send, gb_recv, pa_send, pa_recv, pb_send, pb_recv,
    ta_send, ta_recv, tb_send, tb_recv, ra_send, ra_recv, rb_send, rb_recv, st_send, st_recv,
):
    width = pool_ref.shape[1]
    each = pool_ref.shape[0]
    both = 2 * each
    deep = width + 16
    na, nb = len(FIRST), len(SECOND)
    points = float(each * 128)
    x, y, z, core = place()

    def to_first(a):
        return device(x + a // 2, y, z, core + a % 2)

    def from_first(a):
        return device(x - a // 2, y, z, core + a % 2)

    def to_second(b):
        return device(x, y + pick(b, [v[0] for v in SECOND]), z + pick(b, [v[1] for v in SECOND]), core)

    def from_second(b):
        return device(x, y - pick(b, [v[0] for v in SECOND]), z - pick(b, [v[1] for v in SECOND]), core)

    def copy(src, dst, send, recv, target):
        return pltpu.make_async_remote_copy(
            src_ref=src, dst_ref=dst, send_sem=send, recv_sem=recv, device_id=target, device_id_type=MESH
        )

    first_others = [a for a in range(na) if a != OWN_FIRST]
    second_others = [b for b in range(nb) if b != OWN_SECOND]

    def lanes(index, count=1):
        return pl.ds(pl.multiple_of(index * both * count, both * count), both * count)

    def block_lanes(index):
        return pl.ds(pl.multiple_of(index * both, both), both)

    def gather_first(a):
        return copy(own, at.at[:, block_lanes(a)], ga_send.at[a], ga_recv.at[a], from_first(a))

    def gather_second(b):
        return copy(
            own, bt.at[pl.ds(0, width), block_lanes(b)], gb_send.at[b], gb_recv.at[b], from_second(b)
        )

    def partial_first(a):
        return copy(part_a.at[:, block_lanes(a)], part_in.at[a], pa_send.at[a], pa_recv.at[a], to_first(a))

    def partial_second(b):
        return copy(part_b.at[:, block_lanes(b)], part_in.at[na + b], pb_send.at[b], pb_recv.at[b], to_second(b))

    def total_first(a):
        return copy(t_own, ta.at[:, block_lanes(a)], ta_send.at[a], ta_recv.at[a], from_first(a))

    def total_second(b):
        return copy(t_own, tb.at[:, block_lanes(b)], tb_send.at[b], tb_recv.at[b], from_second(b))

    def return_first(a):
        return copy(ga.at[:, block_lanes(a)], g_in.at[a], ra_send.at[a], ra_recv.at[a], to_first(a))

    def return_second(b):
        return copy(gb.at[:, block_lanes(b)], g_in.at[na + b], rb_send.at[b], rb_recv.at[b], to_second(b))

    def stats(slot):
        target = device(x, y - slot // 4, z - slot % 4, core)
        return copy(stat_out, stat_in.at[slot], st_send.at[slot], st_recv.at[slot], target)

    partners = [(dx, 0, 0, dk) for dx, dk in FIRST if (dx, dk) != (0, 0)]
    partners += [(0, slot // 4, slot % 4, 0) for slot in range(1, 16)]
    barrier = pltpu.get_barrier_semaphore()
    for dx, dy, dz, dk in partners:
        pl.semaphore_signal(
            barrier, inc=1, device_id=device(x + dx, y + dy, z + dz, core + dk), device_id_type=MESH
        )

    sign = jnp.where(lax.broadcasted_iota(jnp.int32, (1, both), 1) < each, 1.0, -1.0).astype(F32)
    rows = jnp.concatenate([pool_ref[...].astype(F32), label_ref[...].astype(F32)], axis=0)
    block = rows.T.astype(BF16)
    own[...] = block
    at[:, pl.ds(OWN_FIRST * both, both)] = block
    bt[0:width, pl.ds(OWN_SECOND * both, both)] = block
    bt[deep:, :] = jnp.zeros((bt.shape[0] - deep, nb * both), BF16)
    acc_a[...] = jnp.zeros(acc_a.shape, F32)
    acc_b[...] = jnp.zeros(acc_b.shape, F32)

    pl.semaphore_wait(barrier, len(partners))

    for b in (0, 1):
        gather_second(b).start()
    for a in (1, 2, 3):
        gather_first(a).start()
    for b in (2, 3):
        gather_second(b).start()
    for a in (6, 7):
        gather_first(a).start()
    for b in (7, 4, 5):
        gather_second(b).start()
    for a in (4, 5):
        gather_first(a).start()
    for b in (8, 9):
        gather_second(b).start()

    place8 = lax.broadcasted_iota(jnp.int32, (8, both), 0)
    none8 = jnp.zeros((8, both), F32)
    ones8 = jnp.where(place8 < 3, 1.0, none8)
    sign8 = jnp.where(place8 == 0, sign, none8)

    def three_rows(parts, start):
        out = none8
        for i, part in enumerate(parts):
            out = jnp.where(place8 == start + i, part, out)
        return out

    def half_norms(value):
        return three_rows(split3(jnp.sum(value * value, axis=0, keepdims=True) * -0.5), 0)

    def take_first(a):
        here = block_lanes(a)
        value = at[:, here].astype(F32)
        za[here, 0:width] = value.T.astype(BF16)
        rest = jnp.concatenate([ones8, half_norms(value), jnp.zeros((width - 16, both), F32)], axis=0)
        za[here, width : 2 * width] = rest.T.astype(BF16)
        w1a[0:width, here] = (value * sign).astype(BF16)
        w1a[width:deep, here] = jnp.concatenate([sign8, none8], axis=0).astype(BF16)

    def take_second(b):
        here = block_lanes(b)
        value = bt[0:width, here].astype(F32)
        bt[width:deep, here] = jnp.concatenate([half_norms(value), ones8], axis=0).astype(BF16)
        wb[0:width, here] = (value * sign).astype(BF16)

    scale = math.log2(math.e) / width
    tile_sign = sign[:, 128:256]

    def order(i):
        return i + jnp.where(i == 2, 1, 0) - jnp.where(i == 3, 1, 0)

    def sum_second(w, out, pair):
        here = lanes(pair, 2)

        @pl.when(pair < TWO_SIDED)
        def _():
            out[:, here] = matmul(w[...], km[:, here])

        @pl.when(pair >= TWO_SIDED)
        def _():
            out[:, here] = matmul(w[:, 2 * both : 4 * both], km[2 * both : 4 * both, here])

    def second_step(i, carry):
        pair = order(i)

        @pl.when(i > 0)
        def _():
            sum_second(w1a, o1b, order(i - 1))

        def await_second(b):
            @pl.when(b != OWN_SECOND)
            def _():
                gather_second(b).wait_recv()

            take_second(b)

        await_second(2 * pair)
        await_second(2 * pair + 1)
        wide = lanes(pair, 2)

        def first_step(ap, carry):
            @pl.when(i == 0)
            def _():
                @pl.when(ap > 0)
                def _():
                    gather_first(2 * ap).wait_recv()

                gather_first(2 * ap + 1).wait_recv()
                take_first(2 * ap)
                take_first(2 * ap + 1)

            here = lanes(ap, 2)
            product = matmul(za[here, :], bt[:, wide])
            value = jnp.exp2(product * scale)
            km[here, wide] = value.astype(BF16)
            tiles = [value[:, 128 * j : 128 * (j + 1)] for j in range(6)]
            across = (tiles[0] - tiles[2]) + (tiles[3] - tiles[5]) + (tiles[1] + tiles[4]) * tile_sign
            acc_a[here, :] += across
            parts = [
                jnp.sum(value[each * j : each * (j + 1)].reshape(each // 8, 8, 2 * both), axis=0) for j in range(4)
            ]
            unused = (pair >= TWO_SIDED) & (ap != 1)
            to = pl.multiple_of(jnp.where(unused, 8, 0), 8)
            acc_b[pl.ds(to, 8), wide] += (parts[0] - parts[1]) + (parts[2] - parts[3])
            return carry

        lax.fori_loop(0, jnp.where(pair < TWO_SIDED, 4, 3), first_step, 0)

        for b in (2 * pair, 2 * pair + 1):
            here = block_lanes(b)
            part_b[:, here] = jnp.broadcast_to(jnp.sum(acc_b[0:8, here], axis=0, keepdims=True) * sign, (8, both))

            @pl.when(b != OWN_SECOND)
            def _():
                partial_second(b).start()

        return carry

    lax.fori_loop(0, SECOND_PAIRS, second_step, 0)

    for a in (4, 5, 2, 3, 6, 7, 1, 0):
        here = pl.ds(a * both, both)
        total = jnp.sum(acc_a[here, :].T, axis=0, keepdims=True) * sign
        part_a[:, here] = jnp.broadcast_to(total, (8, both))
        if a != OWN_FIRST:
            partial_first(a).start()
    sum_second(w1a, o1b, SECOND_PAIRS - 1)

    total = part_a[:, pl.ds(OWN_FIRST * both, both)] + part_b[:, pl.ds(OWN_SECOND * both, both)]
    for b in second_others:
        partial_second(b).wait_recv()
        total = total + part_in[na + b]
    for a in first_others:
        partial_first(a).wait_recv()
        total = total + part_in[a]
    total = total + pltpu.roll(total, each, 1)
    t_own[...] = total
    ta[:, pl.ds(OWN_FIRST * both, both)] = total
    tb[:, pl.ds(OWN_SECOND * both, both)] = total
    for a in first_others:
        total_first(a).start()
    for b in second_others:
        total_second(b).start()
    for a in first_others:
        total_first(a).wait_recv()

    line = ta[0:1, :]
    local = jnp.sum(line, axis=1, keepdims=True) / (na * both)
    spread = 0.5 * jnp.sum(jnp.square(line - local), axis=1, keepdims=True)
    shared = jnp.where(lax.broadcasted_iota(jnp.int32, (8, 128), 1) < 64, local, spread)
    stat_out[...] = shared
    stat_in[0] = shared
    for slot in range(1, 16):
        stats(slot).start()

    def weigh_first(a, carry):
        here = block_lanes(a)
        shifted = ta[0:1, here] - local
        w2a[0:width, here] = (w1a[0:width, here].astype(F32) * shifted).astype(BF16)
        w2a[width:deep, here] = jnp.concatenate([three_rows(split3(shifted * sign), 0), none8], axis=0).astype(BF16)
        return carry

    lax.fori_loop(0, na, weigh_first, 0)

    def sum_second_again(pair, carry):
        sum_second(w2a, o2b, pair)
        return carry

    lax.fori_loop(0, SECOND_PAIRS, sum_second_again, 0)
    for b in second_others:
        total_second(b).wait_recv()

    def weigh_second(b, carry):
        here = block_lanes(b)
        shifted = tb[0:1, here] - local
        wb[width : 2 * width, here] = (wb[0:width, here].astype(F32) * shifted).astype(BF16)
        tail = sign8 + three_rows(split3(shifted * sign), 1)
        wb[2 * width : 2 * width + 16, here] = jnp.concatenate([tail, none8], axis=0).astype(BF16)
        return carry

    lax.fori_loop(0, nb, weigh_second, 0)
    inner = TWO_SIDED * 2 * both
    oa[:, 6 * both : 8 * both] = matmul_t(wb[:, 0:inner], km[6 * both : 8 * both, 0:inner])

    for slot in range(1, 16):
        stats(slot).wait_recv()
    every = stat_in[...]
    added = jnp.sum(every, axis=0)
    mean = added[0:1, 0:1] * (1.0 / 16.0)
    away = jnp.sum(jnp.square(every - mean), axis=0)
    spread = added[0:1, 64:65] + float(na * each) * away[0:1, 0:1]
    variance = 4.0 * spread / points**3 + 1e-08
    statistic = mean / points
    deviation = jnp.sqrt(variance)
    coef_a = 1.0 / (points * deviation)
    coef_b = -4.0 * statistic / (points**2 * (variance * deviation))
    objective_ref[...] = jnp.broadcast_to(statistic / deviation, objective_ref.shape)
    base = 2.0 * coef_a + 2.0 * coef_b * (local - mean)
    outer = sign * (-1.0 / width)

    def combine(value, shifted, plain, rho, weighted, tau):
        alpha = base + coef_b * shifted
        return (value * rho - plain) * (alpha * outer) + (value * tau - weighted) * (coef_b * outer)

    def gradient_first(a):
        here = block_lanes(a)
        low = 2 * width
        tau = oa[low + 1 : low + 2, here] + oa[low + 2 : low + 3, here] + oa[low + 3 : low + 4, here]
        return combine(
            at[:, here].astype(F32), ta[0:1, here] - local,
            oa[0:width, here], oa[low : low + 1, here], oa[width:low, here], tau,
        )

    def gradient_second(b):
        here = block_lanes(b)
        tau = o2b[width : width + 1, here] + o2b[width + 1 : width + 2, here] + o2b[width + 2 : width + 3, here]
        return combine(
            bt[0:width, here].astype(F32), tb[0:1, here] - local,
            o1b[0:width, here], o1b[width : width + 1, here], o2b[0:width, here], tau,
        )

    def finish_second(j, carry):
        b = nb - 1 - j

        @pl.when(b != OWN_SECOND)
        def _():
            gb[:, block_lanes(b)] = gradient_second(b).astype(BF16)
            return_second(b).start()

        return carry

    def finish_first(a):
        ga[:, block_lanes(a)] = gradient_first(a).astype(BF16)
        return_first(a).start()

    lax.fori_loop(0, nb, finish_second, 0)
    finish_first(6)
    finish_first(7)

    def first_sums(j, carry):
        ap = 2 - j
        here = lanes(ap, 2)
        oa[:, here] = matmul_t(wb[...], km[here, :])

        @pl.when(ap > 0)
        def _():
            finish_first(2 * ap)

        finish_first(2 * ap + 1)
        return carry

    lax.fori_loop(0, 3, first_sums, 0)
    result = gradient_first(OWN_FIRST) + gradient_second(OWN_SECOND)
    for a in first_others:
        return_first(a).wait_recv()
        result = result + g_in[a].astype(F32)
    for b in second_others:
        return_second(b).wait_recv()
        result = result + g_in[na + b].astype(F32)
    result = result.T
    grad_pool_ref[...] = result[0:each]
    grad_label_ref[...] = result[each:both]

    for a in first_others:
        for item in (gather_first, partial_first, total_first, return_first):
            item(a).wait_send()
    for b in second_others:
        for item in (gather_second, partial_second, total_second, return_second):
            item(b).wait_send()
    for slot in range(1, 16):
        stats(slot).wait_send()


def shards(pool, labeled):
    each, width = pool.shape
    both = 2 * each
    deep = width + 16
    na, nb = len(FIRST), len(SECOND)
    la, lb = na * both, nb * both
    dma = pltpu.SemaphoreType.DMA
    vmem = pl.BlockSpec(memory_space=pltpu.VMEM)
    scratch = [
        pltpu.VMEM((width, both), BF16),
        pltpu.VMEM((width, la), BF16),
        pltpu.VMEM((2 * width, lb), BF16),
        pltpu.VMEM((la, 2 * width), BF16),
        pltpu.VMEM((la, lb), BF16),
        pltpu.VMEM((la, 128), F32),
        pltpu.VMEM((16, lb), F32),
        pltpu.VMEM((8, la), F32),
        pltpu.VMEM((8, lb), F32),
        pltpu.VMEM((na + nb, 8, both), F32),
        pltpu.VMEM((8, both), F32),
        pltpu.VMEM((8, la), F32),
        pltpu.VMEM((8, lb), F32),
        pltpu.VMEM((deep, la), BF16),
        pltpu.VMEM((deep, la), BF16),
        pltpu.VMEM((width + deep, lb), BF16),
        pltpu.VMEM((deep, lb), F32),
        pltpu.VMEM((deep, lb), F32),
        pltpu.VMEM((width + deep, la), F32),
        pltpu.VMEM((width, la), BF16),
        pltpu.VMEM((width, lb), BF16),
        pltpu.VMEM((na + nb, width, both), BF16),
        pltpu.VMEM((8, 128), F32),
        pltpu.VMEM((16, 8, 128), F32),
    ]
    for _ in range(4):
        scratch += [dma((na,)), dma((na,)), dma((nb,)), dma((nb,))]
    scratch += [dma((16,)), dma((16,))]
    grad_pool, grad_label, objective = pl.pallas_call(
        kernel,
        out_shape=(
            jax.ShapeDtypeStruct((each, width), F32),
            jax.ShapeDtypeStruct((each, width), F32),
            jax.ShapeDtypeStruct((8, 128), F32),
        ),
        in_specs=[vmem, vmem],
        out_specs=(vmem, vmem, vmem),
        scratch_shapes=scratch,
        compiler_params=pltpu.CompilerParams(
            collective_id=0, has_side_effects=True, vmem_limit_bytes=60 * 2**20
        ),
    )(pool, labeled)
    return grad_pool, grad_label, objective[0, 0]


def solution(mesh):
    in_specs = (P(("row", "col"), None), P(("row", "col"), None))
    out_specs = (P(("row", "col"), None), P(("row", "col"), None), P())
    return jax.shard_map(shards, mesh=mesh, in_specs=in_specs, out_specs=out_specs, check_vma=False)
```

```python
import math

import jax
import jax.numpy as jnp
from jax import lax
from jax.experimental import pallas as pl
from jax.experimental.pallas import tpu as pltpu
from jax.sharding import PartitionSpec as P

MESH = pl.DeviceIdType.MESH
F32 = jnp.float32
BF16 = jnp.bfloat16

FIRST = tuple((dx, dk) for dx in range(4) for dk in range(2))
SECOND = ((0, 1), (-1, 0), (1, 1), (-1, 1), (1, 2), (2, -1), (0, 0), (0, 2), (2, 0), (2, 2))
OWN_FIRST = FIRST.index((0, 0))
OWN_SECOND = SECOND.index((0, 0))
RELAY = {
    0: ((0, 1), (0, 1)),
    1: ((-1, 0), (-1, 0)),
    2: ((1, 0), (1, 0)),
    3: ((-1, 0), (0, 1)),
    7: ((0, 1), (0, 1)),
    8: ((-1, 0), (-1, 0)),
    4: ((1, 0), (1, 0)),
    5: ((0, -1), (0, -1)),
    9: ((-1, 1), (-1, 1)),
}
TWO_SIDED = 3
SECOND_PAIRS = len(SECOND) // 2


def place():
    row, col = lax.axis_index("row"), lax.axis_index("col")
    return ((col // 2) % 2) * 2 + row // 4, col // 4, row % 4, col % 2


def device(x, y, z, core):
    x, y, z, core = (x + 8) % 4, (y + 8) % 4, (z + 8) % 4, (core + 2) % 2
    return ((x % 2) * 4 + z, y * 4 + (x // 2) * 2 + core)


def split3(value):
    high = value.astype(BF16).astype(F32)
    rest = value - high
    middle = rest.astype(BF16).astype(F32)
    return high, middle, rest - middle


def matmul(left, right):
    return lax.dot_general(left, right, (((1,), (0,)), ((), ())), preferred_element_type=F32)


def matmul_t(left, right):
    return lax.dot_general(left, right, (((1,), (1,)), ((), ())), preferred_element_type=F32)


def pick(index, values):
    out = values[-1]
    for i in range(len(values) - 2, -1, -1):
        out = jnp.where(index == i, values[i], out)
    return out


def kernel(
    pool_ref, label_ref, grad_pool_ref, grad_label_ref, objective_ref,
    own, at, bt, za, km, acc_a, acc_b, part_a, part_b, first_in, second_in, sum_b, sum_b_in, t_own, ta, tb,
    w1a, w2a, wb, o1b, o2b, oa, ga, gb, g_in, stat_out, stat_in,
    ga_send, ga_recv, gb_send, gb_recv, pa_send, pa_recv, pb_send, pb_recv,
    ta_send, ta_recv, tb_send, tb_recv, ra_send, ra_recv, rb_send, rb_recv, st_send, st_recv,
):
    width = pool_ref.shape[1]
    each = pool_ref.shape[0]
    both = 2 * each
    deep = width + 16
    na, nb = len(FIRST), len(SECOND)
    points = float(each * 128)
    x, y, z, core = place()

    def to_first(a):
        return device(x + a // 2, y, z, core + a % 2)

    def from_first(a):
        return device(x - a // 2, y, z, core + a % 2)

    def to_second(b):
        return device(x, y + pick(b, [v[0] for v in SECOND]), z + pick(b, [v[1] for v in SECOND]), core)

    def from_second(b):
        return device(x, y - pick(b, [v[0] for v in SECOND]), z - pick(b, [v[1] for v in SECOND]), core)

    def copy(src, dst, send, recv, target):
        return pltpu.make_async_remote_copy(
            src_ref=src, dst_ref=dst, send_sem=send, recv_sem=recv, device_id=target, device_id_type=MESH
        )

    first_others = [a for a in range(na) if a != OWN_FIRST]
    second_others = [b for b in range(nb) if b != OWN_SECOND]
    shared = range(2 * TWO_SIDED)

    def lanes(index, count=1):
        return pl.ds(pl.multiple_of(index * both * count, both * count), both * count)

    def block_lanes(index):
        return pl.ds(pl.multiple_of(index * both, both), both)

    def gather_first(a):
        return copy(own, at.at[:, block_lanes(a)], ga_send.at[a], ga_recv.at[a], from_first(a))

    def forward(a):
        return copy(
            at.at[:, block_lanes(a - 1)], at.at[:, block_lanes(a)], ga_send.at[a], ga_recv.at[a],
            device(x, y, z, core + 1),
        )

    def gather_second(b):
        if b in (0, 1):
            source = own
        else:
            at_neighbour = {2: 0, 3: jnp.where(core == 0, 0, 1), 4: 7, 5: 8, 7: 0, 8: 1, 9: 3}[b]
            source = bt.at[pl.ds(0, width), block_lanes(at_neighbour)]
        first, other = RELAY[b]
        dy = jnp.where(core == 0, first[0], other[0])
        dz = jnp.where(core == 0, first[1], other[1])
        return copy(
            source, bt.at[pl.ds(0, width), block_lanes(b)], gb_send.at[b], gb_recv.at[b],
            device(x, y - dy, z - dz, core),
        )

    def partial_first(a):
        return copy(part_a, first_in.at[a], pa_send.at[a], pa_recv.at[a], from_first(a))

    def partial_second(b):
        return copy(part_b.at[:, block_lanes(b)], second_in.at[b], pb_send.at[b], pb_recv.at[b], to_second(b))

    def total_first(a):
        return copy(sum_b, sum_b_in.at[a], ta_send.at[a], ta_recv.at[a], from_first(a))

    def total_second(b):
        return copy(t_own, tb.at[:, block_lanes(b)], tb_send.at[b], tb_recv.at[b], from_second(b))

    def return_first(a):
        return copy(ga.at[:, block_lanes(a)], g_in.at[a], ra_send.at[a], ra_recv.at[a], to_first(a))

    def return_second(b):
        return copy(gb.at[:, block_lanes(b)], g_in.at[na + b], rb_send.at[b], rb_recv.at[b], to_second(b))

    def stats(slot):
        target = device(x, y - slot // 4, z - slot % 4, core)
        return copy(stat_out, stat_in.at[slot], st_send.at[slot], st_recv.at[slot], target)

    partners = [(dx, 0, 0, dk) for dx, dk in FIRST if (dx, dk) != (0, 0)]
    partners += [(0, slot // 4, slot % 4, 0) for slot in range(1, 16)]
    barrier = pltpu.get_barrier_semaphore()
    for dx, dy, dz, dk in partners:
        pl.semaphore_signal(
            barrier, inc=1, device_id=device(x + dx, y + dy, z + dz, core + dk), device_id_type=MESH
        )

    sign = jnp.where(lax.broadcasted_iota(jnp.int32, (1, both), 1) < each, 1.0, -1.0).astype(F32)
    rows = jnp.concatenate([pool_ref[...].astype(F32), label_ref[...].astype(F32)], axis=0)
    block = rows.T.astype(BF16)
    own[...] = block
    at[:, pl.ds(OWN_FIRST * both, both)] = block
    bt[0:width, pl.ds(OWN_SECOND * both, both)] = block
    bt[deep:, :] = jnp.zeros((bt.shape[0] - deep, nb * both), BF16)
    acc_a[...] = jnp.zeros(acc_a.shape, F32)
    acc_b[...] = jnp.zeros(acc_b.shape, F32)

    pl.semaphore_wait(barrier, len(partners))

    for a in (2, 6, 1):
        gather_first(a).start()
    for b in (0, 1):
        gather_second(b).start()
    gather_first(4).start()

    place8 = lax.broadcasted_iota(jnp.int32, (8, both), 0)
    none8 = jnp.zeros((8, both), F32)
    ones8 = jnp.where(place8 < 3, 1.0, none8)
    sign8 = jnp.where(place8 == 0, sign, none8)

    def three_rows(parts, start):
        out = none8
        for i, part in enumerate(parts):
            out = jnp.where(place8 == start + i, part, out)
        return out

    def half_norms(value):
        return three_rows(split3(jnp.sum(value * value, axis=0, keepdims=True) * -0.5), 0)

    def take_first(a):
        here = block_lanes(a)
        value = at[:, here].astype(F32)
        za[here, 0:width] = value.T.astype(BF16)
        rest = jnp.concatenate([ones8, half_norms(value), jnp.zeros((width - 16, both), F32)], axis=0)
        za[here, width : 2 * width] = rest.T.astype(BF16)
        w1a[0:width, here] = (value * sign).astype(BF16)
        w1a[width:deep, here] = jnp.concatenate([sign8, none8], axis=0).astype(BF16)

    def take_second(b):
        here = block_lanes(b)
        value = bt[0:width, here].astype(F32)
        bt[width:deep, here] = jnp.concatenate([half_norms(value), ones8], axis=0).astype(BF16)
        wb[0:width, here] = (value * sign).astype(BF16)

    scale = math.log2(math.e) / width
    tile_sign = sign[:, 128:256]

    def sum_second(w, out):
        def body(pair, carry):
            here = lanes(pair, 2)
            out[:, here] = matmul(w[...], km[:, here])
            return carry

        lax.fori_loop(0, TWO_SIDED, body, 0)

    def turn(expected, following):
        for b in expected:
            gather_second(b).wait_recv()
        for b in following:
            gather_second(b).start()

    def once(t, steps, action):
        chosen = t == steps[0]
        for step in steps[1:]:
            chosen = chosen | (t == step)
        pl.when(chosen)(action)

    def kernel_step(t, carry):
        late = t - 8
        pair = jnp.where(t < 3, 0, jnp.where(t < 6, 1, jnp.where(t < 8, t - 6, pick(late // 4, (3, 2, 4)))))
        ap = jnp.where(t < 6, pick(t % 3, (0, 1, 3)), jnp.where(t < 8, 2, late % 4))

        def relay_first(a):
            gather_first(a).wait_recv()
            forward(a + 1).start()

        once(t, (0,), lambda: turn((0, 1), (2, 3, 7, 8)))
        once(t, (3,), lambda: turn((2, 3, 7, 8), (4, 5, 9)))
        once(t, (12,), lambda: turn((4, 5), ()))
        once(t, (16,), lambda: turn((9,), ()))
        once(t, (0,), lambda: relay_first(2))
        once(t, (1,), lambda: relay_first(6))
        once(t, (4,), lambda: relay_first(4))

        def new_second():
            take_second(2 * pair)
            take_second(2 * pair + 1)

        def new_first():
            gather_first(2 * ap + 1).wait_recv()
            take_first(2 * ap)
            take_first(2 * ap + 1)

        once(t, (0, 3, 8, 12, 16), new_second)
        once(t, (0, 1, 2, 6), new_first)
        wide = lanes(pair, 2)
        here = lanes(ap, 2)
        product = matmul(za[here, :], bt[:, wide])
        value = jnp.exp2(product * scale)
        km[here, wide] = value.astype(BF16)
        tiles = [value[:, 128 * j : 128 * (j + 1)] for j in range(6)]
        across = (tiles[0] - tiles[2]) + (tiles[3] - tiles[5]) + (tiles[1] + tiles[4]) * tile_sign
        acc_a[here, :] += across
        parts = [
            jnp.sum(value[each * j : each * (j + 1)].reshape(each // 8, 8, 2 * both), axis=0) for j in range(4)
        ]
        acc_b[:, lanes(jnp.minimum(pair, TWO_SIDED), 2)] += (parts[0] - parts[1]) + (parts[2] - parts[3])

        def second_done():
            for b in (2 * pair, 2 * pair + 1):
                here = block_lanes(b)
                total = jnp.sum(acc_b[:, here], axis=0, keepdims=True) * sign
                part_b[:, here] = jnp.broadcast_to(total, (8, both))
                partial_second(b).start()

        once(t, (6, 7, 15), second_done)
        return carry

    lax.fori_loop(0, 4 * SECOND_PAIRS, kernel_step, 0)

    rows8 = none8
    for a in range(na):
        rows8 = jnp.where(place8 == a, jnp.sum(acc_a[a * both : (a + 1) * both, :].T, axis=0, keepdims=True), rows8)
    part_a[...] = rows8 * sign
    for a in first_others:
        partial_first(a).start()
    got = none8
    for b in shared:
        partial_second(b).wait_recv()
        got = got + second_in[b]
    sum_b[...] = got
    for a in first_others:
        total_first(a).start()
    sum_second(w1a, o1b)

    def seen_from(value, a):
        dx, dk = FIRST[a]
        if dk:
            value = jnp.where(place8 % 2 == 0, pltpu.roll(value, 7, 0), pltpu.roll(value, 1, 0))
        return pltpu.roll(value, 2 * dx, 0) if dx else value

    total = part_a[...]
    for a in first_others:
        partial_first(a).wait_recv()
        total = total + seen_from(first_in[a], a)
    total = total + jnp.where(place8 == OWN_FIRST, got, 0.0)
    for a in first_others:
        total_first(a).wait_recv()
        total = total + jnp.where(place8 == a, sum_b_in[a], 0.0)
    total = total + pltpu.roll(total, each, 1)
    for a in range(na):
        ta[:, a * both : (a + 1) * both] = jnp.broadcast_to(total[a : a + 1], (8, both))
    mine = jnp.broadcast_to(total[OWN_FIRST : OWN_FIRST + 1], (8, both))
    t_own[...] = mine
    tb[:, pl.ds(OWN_SECOND * both, both)] = mine
    for b in second_others:
        total_second(b).start()

    line = ta[0:1, :]
    local = jnp.sum(line, axis=1, keepdims=True) / (na * both)
    spread = 0.5 * jnp.sum(jnp.square(line - local), axis=1, keepdims=True)
    told = jnp.where(lax.broadcasted_iota(jnp.int32, (8, 128), 1) < 64, local, spread)
    stat_out[...] = told
    stat_in[0] = told
    for slot in range(1, 16):
        stats(slot).start()

    def weigh_first(a, carry):
        here = block_lanes(a)
        shifted = ta[0:1, here] - local
        w2a[0:width, here] = (w1a[0:width, here].astype(F32) * shifted).astype(BF16)
        w2a[width:deep, here] = jnp.concatenate([three_rows(split3(shifted * sign), 0), none8], axis=0).astype(BF16)
        return carry

    lax.fori_loop(0, na, weigh_first, 0)

    sum_second(w2a, o2b)
    for b in second_others:
        total_second(b).wait_recv()

    def weigh_second(b, carry):
        here = block_lanes(b)
        shifted = tb[0:1, here] - local
        wb[width : 2 * width, here] = (wb[0:width, here].astype(F32) * shifted).astype(BF16)
        tail = sign8 + three_rows(split3(shifted * sign), 1)
        wb[2 * width : 2 * width + 16, here] = jnp.concatenate([tail, none8], axis=0).astype(BF16)
        return carry

    lax.fori_loop(0, nb, weigh_second, 0)

    def first_sums(ap, carry):
        here = lanes(ap, 2)
        oa[:, here] = matmul_t(wb[...], km[here, :])
        return carry

    first_sums(3, 0)
    for slot in range(1, 16):
        stats(slot).wait_recv()
    every = stat_in[...]
    added = jnp.sum(every, axis=0)
    mean = added[0:1, 0:1] * (1.0 / 16.0)
    away = jnp.sum(jnp.square(every - mean), axis=0)
    spread = added[0:1, 64:65] + float(na * each) * away[0:1, 0:1]
    variance = 4.0 * spread / points**3 + 1e-08
    statistic = mean / points
    deviation = jnp.sqrt(variance)
    coef_a = 1.0 / (points * deviation)
    coef_b = -4.0 * statistic / (points**2 * (variance * deviation))
    objective_ref[...] = jnp.broadcast_to(statistic / deviation, objective_ref.shape)
    base = 2.0 * coef_a + 2.0 * coef_b * (local - mean)
    outer = sign * (-1.0 / width)

    def combine(value, shifted, plain, rho, weighted, tau):
        alpha = base + coef_b * shifted
        return (value * rho - plain) * (alpha * outer) + (value * tau - weighted) * (coef_b * outer)

    def gradient_first(a):
        here = block_lanes(a)
        low = 2 * width
        tau = oa[low + 1 : low + 2, here] + oa[low + 2 : low + 3, here] + oa[low + 3 : low + 4, here]
        return combine(
            at[:, here].astype(F32), ta[0:1, here] - local,
            oa[0:width, here], oa[low : low + 1, here], oa[width:low, here], tau,
        )

    def gradient_second(b):
        here = block_lanes(b)
        tau = o2b[width : width + 1, here] + o2b[width + 1 : width + 2, here] + o2b[width + 2 : width + 3, here]
        return combine(
            bt[0:width, here].astype(F32), tb[0:1, here] - local,
            o1b[0:width, here], o1b[width : width + 1, here], o2b[0:width, here], tau,
        )

    def finish_second(j, carry):
        b = 2 * TWO_SIDED - 1 - j
        gb[:, block_lanes(b)] = gradient_second(b).astype(BF16)
        return_second(b).start()
        return carry

    def finish_first(a):
        ga[:, block_lanes(a)] = gradient_first(a).astype(BF16)
        return_first(a).start()

    def finish_and_sum(j, carry):
        ap = 3 - j
        finish_first(2 * ap)
        finish_first(2 * ap + 1)

        @pl.when(j == 0)
        def _():
            lax.fori_loop(0, 2 * TWO_SIDED, finish_second, 0)

        first_sums(ap - 1, 0)
        return carry

    lax.fori_loop(0, 3, finish_and_sum, 0)
    finish_first(1)
    result = gradient_first(OWN_FIRST)
    for a in first_others:
        return_first(a).wait_recv()
        result = result + g_in[a].astype(F32)
    for b in shared:
        return_second(b).wait_recv()
        result = result + g_in[na + b].astype(F32)
    result = result.T
    grad_pool_ref[...] = result[0:each]
    grad_label_ref[...] = result[each:both]

    for a in first_others:
        for item in (gather_first if a in (1, 2, 4, 6) else forward, partial_first, total_first, return_first):
            item(a).wait_send()
    for b in second_others:
        for item in (gather_second, total_second):
            item(b).wait_send()
    for b in shared:
        for item in (partial_second, return_second):
            item(b).wait_send()
    for slot in range(1, 16):
        stats(slot).wait_send()


def shards(pool, labeled):
    each, width = pool.shape
    both = 2 * each
    deep = width + 16
    na, nb = len(FIRST), len(SECOND)
    la, lb, ls = na * both, nb * both, 2 * TWO_SIDED * both
    dma = pltpu.SemaphoreType.DMA
    vmem = pl.BlockSpec(memory_space=pltpu.VMEM)
    scratch = [
        pltpu.VMEM((width, both), BF16),
        pltpu.VMEM((width, la), BF16),
        pltpu.VMEM((2 * width, lb), BF16),
        pltpu.VMEM((la, 2 * width), BF16),
        pltpu.VMEM((la, lb), BF16),
        pltpu.VMEM((la, 128), F32),
        pltpu.VMEM((8, ls + 2 * both), F32),
        pltpu.VMEM((8, both), F32),
        pltpu.VMEM((8, ls), F32),
        pltpu.VMEM((na, 8, both), F32),
        pltpu.VMEM((2 * TWO_SIDED, 8, both), F32),
        pltpu.VMEM((8, both), F32),
        pltpu.VMEM((na, 8, both), F32),
        pltpu.VMEM((8, both), F32),
        pltpu.VMEM((8, la), F32),
        pltpu.VMEM((8, lb), F32),
        pltpu.VMEM((deep, la), BF16),
        pltpu.VMEM((deep, la), BF16),
        pltpu.VMEM((width + deep, lb), BF16),
        pltpu.VMEM((deep, ls), F32),
        pltpu.VMEM((deep, ls), F32),
        pltpu.VMEM((width + deep, la), F32),
        pltpu.VMEM((width, la), BF16),
        pltpu.VMEM((width, ls), BF16),
        pltpu.VMEM((na + nb, width, both), BF16),
        pltpu.VMEM((8, 128), F32),
        pltpu.VMEM((16, 8, 128), F32),
    ]
    for _ in range(4):
        scratch += [dma((na,)), dma((na,)), dma((nb,)), dma((nb,))]
    scratch += [dma((16,)), dma((16,))]
    grad_pool, grad_label, objective = pl.pallas_call(
        kernel,
        out_shape=(
            jax.ShapeDtypeStruct((each, width), F32),
            jax.ShapeDtypeStruct((each, width), F32),
            jax.ShapeDtypeStruct((8, 128), F32),
        ),
        in_specs=[vmem, vmem],
        out_specs=(vmem, vmem, vmem),
        scratch_shapes=scratch,
        compiler_params=pltpu.CompilerParams(
            collective_id=0, has_side_effects=True, vmem_limit_bytes=60 * 2**20
        ),
    )(pool, labeled)

    def hand_on(pool_in, label_in, objective_in, pool_out, label_out, objective_out):
        pool_out[...] = pool_in[...]
        label_out[...] = label_in[...]
        objective_out[0, 0] = objective_in[0, 0]

    grad_pool, grad_label, objective = pl.pallas_call(
        hand_on,
        out_shape=(
            jax.ShapeDtypeStruct((each, width), F32),
            jax.ShapeDtypeStruct((each, width), F32),
            jax.ShapeDtypeStruct((1, 1), F32),
        ),
        in_specs=[vmem, vmem, vmem],
        out_specs=(vmem, vmem, pl.BlockSpec(memory_space=pltpu.SMEM)),
    )(grad_pool, grad_label, objective)
    return grad_pool, grad_label, objective.reshape(())


def solution(mesh):
    in_specs = (P(("row", "col"), None), P(("row", "col"), None))
    out_specs = (P(("row", "col"), None), P(("row", "col"), None), P())
    return jax.shard_map(shards, mesh=mesh, in_specs=in_specs, out_specs=out_specs, check_vma=False)
```

```python
import math

import jax
import jax.numpy as jnp
from jax import lax
from jax.experimental import pallas as pl
from jax.experimental.pallas import tpu as pltpu
from jax.sharding import PartitionSpec as P

MESH = pl.DeviceIdType.MESH
F32 = jnp.float32
BF16 = jnp.bfloat16

FIRST = tuple((dx, dk) for dx in range(4) for dk in range(2))
SECOND = ((0, 1), (-1, 0), (1, 1), (-1, 1), (1, 2), (2, -1), (0, 0), (0, 2), (2, 0), (2, 2))
OWN_FIRST = FIRST.index((0, 0))
OWN_SECOND = SECOND.index((0, 0))
RELAY = {
    0: ((0, 1), (0, 1)),
    1: ((-1, 0), (-1, 0)),
    2: ((1, 0), (1, 0)),
    3: ((-1, 0), (0, 1)),
    7: ((0, 1), (0, 1)),
    8: ((-1, 0), (-1, 0)),
    4: ((1, 0), (1, 0)),
    5: ((0, -1), (0, -1)),
    9: ((0, 2), (2, 0)),
}
TWO_SIDED = 3
SECOND_PAIRS = len(SECOND) // 2


def place():
    row, col = lax.axis_index("row"), lax.axis_index("col")
    return ((col // 2) % 2) * 2 + row // 4, col // 4, row % 4, col % 2


def device(x, y, z, core):
    x, y, z, core = (x + 8) % 4, (y + 8) % 4, (z + 8) % 4, (core + 2) % 2
    return ((x % 2) * 4 + z, y * 4 + (x // 2) * 2 + core)


def split3(value):
    high = value.astype(BF16).astype(F32)
    rest = value - high
    middle = rest.astype(BF16).astype(F32)
    return high, middle, rest - middle


def matmul(left, right):
    return lax.dot_general(left, right, (((1,), (0,)), ((), ())), preferred_element_type=F32)


def matmul_t(left, right):
    return lax.dot_general(left, right, (((1,), (1,)), ((), ())), preferred_element_type=F32)


def pick(index, values):
    out = values[-1]
    for i in range(len(values) - 2, -1, -1):
        out = jnp.where(index == i, values[i], out)
    return out


def kernel(
    pool_ref, label_ref, grad_pool_ref, grad_label_ref, objective_ref,
    rows_in, own, at, bt, za, km, acc_a, acc_b, part_a, part_b, first_in, second_in, sum_b, sum_b_in, t_own, ta, tb,
    w1a, w2a, wb, o1b, o2b, oa, ga, gb, g_in, stat_out, stat_in,
    ga_send, ga_recv, gb_send, gb_recv, pa_send, pa_recv, pb_send, pb_recv,
    ta_send, ta_recv, tb_send, tb_recv, ra_send, ra_recv, rb_send, rb_recv, st_send, st_recv, read_sem,
):
    width = pool_ref.shape[1]
    each = pool_ref.shape[0]
    both = 2 * each
    deep = width + 16
    na, nb = len(FIRST), len(SECOND)
    points = float(each * 128)
    x, y, z, core = place()

    def to_first(a):
        return device(x + a // 2, y, z, core + a % 2)

    def from_first(a):
        return device(x - a // 2, y, z, core + a % 2)

    def to_second(b):
        return device(x, y + pick(b, [v[0] for v in SECOND]), z + pick(b, [v[1] for v in SECOND]), core)

    def from_second(b):
        return device(x, y - pick(b, [v[0] for v in SECOND]), z - pick(b, [v[1] for v in SECOND]), core)

    def copy(src, dst, send, recv, target):
        return pltpu.make_async_remote_copy(
            src_ref=src, dst_ref=dst, send_sem=send, recv_sem=recv, device_id=target, device_id_type=MESH
        )

    first_others = [a for a in range(na) if a != OWN_FIRST]
    second_others = [b for b in range(nb) if b != OWN_SECOND]
    shared = range(2 * TWO_SIDED)

    def lanes(index, count=1):
        return pl.ds(pl.multiple_of(index * both * count, both * count), both * count)

    def block_lanes(index):
        return pl.ds(pl.multiple_of(index * both, both), both)

    def gather_first(a):
        return copy(own, at.at[:, block_lanes(a)], ga_send.at[a], ga_recv.at[a], from_first(a))

    def forward(a):
        return copy(
            at.at[:, block_lanes(a - 1)], at.at[:, block_lanes(a)], ga_send.at[a], ga_recv.at[a],
            device(x, y, z, core + 1),
        )

    def gather_second(b):
        if b in (0, 1):
            source = own
        else:
            at_neighbour = {2: 0, 3: jnp.where(core == 0, 0, 1), 4: 7, 5: 8, 7: 0, 8: 1, 9: jnp.where(core == 0, 8, 7)}[b]
            source = bt.at[pl.ds(0, width), block_lanes(at_neighbour)]
        first, other = RELAY[b]
        dy = jnp.where(core == 0, first[0], other[0])
        dz = jnp.where(core == 0, first[1], other[1])
        return copy(
            source, bt.at[pl.ds(0, width), block_lanes(b)], gb_send.at[b], gb_recv.at[b],
            device(x, y - dy, z - dz, core),
        )

    def partial_first(a):
        return copy(part_a, first_in.at[a], pa_send.at[a], pa_recv.at[a], from_first(a))

    def partial_second(b):
        return copy(part_b.at[:, block_lanes(b)], second_in.at[b], pb_send.at[b], pb_recv.at[b], to_second(b))

    def total_first(a):
        return copy(sum_b, sum_b_in.at[a], ta_send.at[a], ta_recv.at[a], from_first(a))

    def total_second(b):
        return copy(t_own, tb.at[:, block_lanes(b)], tb_send.at[b], tb_recv.at[b], from_second(b))

    def return_first(a):
        return copy(ga.at[:, block_lanes(a)], g_in.at[a], ra_send.at[a], ra_recv.at[a], to_first(a))

    def return_second(b):
        return copy(gb.at[:, block_lanes(b)], g_in.at[na + b], rb_send.at[b], rb_recv.at[b], to_second(b))

    def stats(slot):
        target = device(x, y - slot // 4, z - slot % 4, core)
        return copy(stat_out, stat_in.at[slot], st_send.at[slot], st_recv.at[slot], target)

    partners = [(0, 0, 0, 1), (1, 0, 0, 0), (3, 0, 0, 0), (2, 0, 0, 0)]
    partners += [(0, 1, 0, 0), (0, 3, 0, 0), (0, 0, 1, 0), (0, 0, 3, 0)]
    barrier = pltpu.get_barrier_semaphore()
    for dx, dy, dz, dk in partners:
        pl.semaphore_signal(
            barrier, inc=1, device_id=device(x + dx, y + dy, z + dz, core + dk), device_id_type=MESH
        )

    reads = [
        pltpu.make_async_copy(pool_ref, rows_in.at[pl.ds(0, each)], read_sem.at[0]),
        pltpu.make_async_copy(label_ref, rows_in.at[pl.ds(each, each)], read_sem.at[1]),
    ]
    for item in reads:
        item.start()
    sign = jnp.where(lax.broadcasted_iota(jnp.int32, (1, both), 1) < each, 1.0, -1.0).astype(F32)
    for item in reads:
        item.wait()
    rows = rows_in[...].astype(F32)
    block = rows.T.astype(BF16)
    own[...] = block
    at[:, pl.ds(OWN_FIRST * both, both)] = block
    bt[0:width, pl.ds(OWN_SECOND * both, both)] = block
    bt[deep:, :] = jnp.zeros((bt.shape[0] - deep, nb * both), BF16)
    acc_a[...] = jnp.zeros(acc_a.shape, F32)
    acc_b[...] = jnp.zeros(acc_b.shape, F32)

    pl.semaphore_wait(barrier, len(partners))

    for a in (2, 6, 1):
        gather_first(a).start()
    for b in (0, 1):
        gather_second(b).start()
    gather_first(4).start()

    place8 = lax.broadcasted_iota(jnp.int32, (8, both), 0)
    none8 = jnp.zeros((8, both), F32)
    ones8 = jnp.where(place8 < 3, 1.0, none8)
    sign8 = jnp.where(place8 == 0, sign, none8)

    def three_rows(parts, start):
        out = none8
        for i, part in enumerate(parts):
            out = jnp.where(place8 == start + i, part, out)
        return out

    def half_norms(value):
        return three_rows(split3(jnp.sum(value * value, axis=0, keepdims=True) * -0.5), 0)

    def take_first(a):
        here = block_lanes(a)
        value = at[:, here].astype(F32)
        za[here, 0:width] = value.T.astype(BF16)
        rest = jnp.concatenate([ones8, half_norms(value), jnp.zeros((width - 16, both), F32)], axis=0)
        za[here, width : 2 * width] = rest.T.astype(BF16)
        w1a[0:width, here] = (value * sign).astype(BF16)
        w1a[width:deep, here] = jnp.concatenate([sign8, none8], axis=0).astype(BF16)

    def take_second(b):
        here = block_lanes(b)
        value = bt[0:width, here].astype(F32)
        bt[width:deep, here] = jnp.concatenate([half_norms(value), ones8], axis=0).astype(BF16)
        wb[0:width, here] = (value * sign).astype(BF16)

    scale = math.log2(math.e) / width
    tile_sign = sign[:, 128:256]

    def sum_second(w, out):
        def body(pair, carry):
            here = lanes(pair, 2)
            out[:, here] = matmul(w[...], km[:, here])
            return carry

        lax.fori_loop(0, TWO_SIDED, body, 0)

    def turn(expected, following):
        for b in expected:
            gather_second(b).wait_recv()
        for b in following:
            gather_second(b).start()

    def once(t, steps, action):
        chosen = t == steps[0]
        for step in steps[1:]:
            chosen = chosen | (t == step)
        pl.when(chosen)(action)

    def kernel_step(t, carry):
        late = t - 8
        pair = jnp.where(t < 3, 0, jnp.where(t < 6, 1, jnp.where(t < 8, t - 6, pick(late // 4, (3, 2, 4)))))
        ap = jnp.where(t < 6, pick(t % 3, (0, 1, 3)), jnp.where(t < 8, 2, late % 4))

        def relay_first(a):
            gather_first(a).wait_recv()
            forward(a + 1).start()

        once(t, (0,), lambda: turn((0, 1), (2, 3, 7, 8)))
        once(t, (3,), lambda: turn((2, 3, 7, 8), (4, 5, 9)))
        once(t, (12,), lambda: turn((4, 5), ()))
        once(t, (16,), lambda: turn((9,), ()))
        once(t, (0,), lambda: relay_first(2))
        once(t, (1,), lambda: relay_first(6))
        once(t, (4,), lambda: relay_first(4))

        def new_second():
            take_second(2 * pair)
            take_second(2 * pair + 1)

        def new_first():
            gather_first(2 * ap + 1).wait_recv()
            take_first(2 * ap)
            take_first(2 * ap + 1)

        once(t, (0, 3, 8, 12, 16), new_second)
        once(t, (0, 1, 2, 6), new_first)
        wide = lanes(pair, 2)
        here = lanes(ap, 2)
        product = matmul(za[here, :], bt[:, wide])
        value = jnp.exp2(product * scale)
        km[here, wide] = value.astype(BF16)
        tiles = [value[:, 128 * j : 128 * (j + 1)] for j in range(6)]
        across = (tiles[0] - tiles[2]) + (tiles[3] - tiles[5]) + (tiles[1] + tiles[4]) * tile_sign
        acc_a[here, :] += across
        parts = [
            jnp.sum(value[each * j : each * (j + 1)].reshape(each // 8, 8, 2 * both), axis=0) for j in range(4)
        ]
        acc_b[:, lanes(jnp.minimum(pair, TWO_SIDED), 2)] += (parts[0] - parts[1]) + (parts[2] - parts[3])

        def second_done():
            for b in (2 * pair, 2 * pair + 1):
                here = block_lanes(b)
                total = jnp.sum(acc_b[:, here], axis=0, keepdims=True) * sign
                part_b[:, here] = jnp.broadcast_to(total, (8, both))
                partial_second(b).start()

        once(t, (6, 7, 15), second_done)
        return carry

    lax.fori_loop(0, 4 * SECOND_PAIRS, kernel_step, 0)

    rows8 = none8
    for a in range(na):
        rows8 = jnp.where(place8 == a, jnp.sum(acc_a[a * both : (a + 1) * both, :].T, axis=0, keepdims=True), rows8)
    part_a[...] = rows8 * sign
    for a in first_others:
        partial_first(a).start()
    got = none8
    for b in shared:
        partial_second(b).wait_recv()
        got = got + second_in[b]
    sum_b[...] = got
    for a in first_others:
        total_first(a).start()
    sum_second(w1a, o1b)

    def seen_from(value, a):
        dx, dk = FIRST[a]
        if dk:
            value = jnp.where(place8 % 2 == 0, pltpu.roll(value, 7, 0), pltpu.roll(value, 1, 0))
        return pltpu.roll(value, 2 * dx, 0) if dx else value

    total = part_a[...]
    for a in first_others:
        partial_first(a).wait_recv()
        total = total + seen_from(first_in[a], a)
    total = total + jnp.where(place8 == OWN_FIRST, got, 0.0)
    for a in first_others:
        total_first(a).wait_recv()
        total = total + jnp.where(place8 == a, sum_b_in[a], 0.0)
    total = total + pltpu.roll(total, each, 1)
    for a in range(na):
        ta[:, a * both : (a + 1) * both] = jnp.broadcast_to(total[a : a + 1], (8, both))
    mine = jnp.broadcast_to(total[OWN_FIRST : OWN_FIRST + 1], (8, both))
    t_own[...] = mine
    tb[:, pl.ds(OWN_SECOND * both, both)] = mine
    for b in (9, 4, 5, 8, 7, 3, 2, 1, 0):
        total_second(b).start()

    line = ta[0:1, :]
    local = jnp.sum(line, axis=1, keepdims=True) / (na * both)
    spread = 0.5 * jnp.sum(jnp.square(line - local), axis=1, keepdims=True)
    told = jnp.where(lax.broadcasted_iota(jnp.int32, (8, 128), 1) < 64, local, spread)
    stat_out[...] = told
    stat_in[0] = told
    for slot in range(1, 16):
        stats(slot).start()

    def weigh_first(a, carry):
        here = block_lanes(a)
        shifted = ta[0:1, here] - local
        w2a[0:width, here] = (w1a[0:width, here].astype(F32) * shifted).astype(BF16)
        w2a[width:deep, here] = jnp.concatenate([three_rows(split3(shifted * sign), 0), none8], axis=0).astype(BF16)
        return carry

    lax.fori_loop(0, na, weigh_first, 0)

    sum_second(w2a, o2b)
    for b in second_others:
        total_second(b).wait_recv()

    def weigh_second(b, carry):
        here = block_lanes(b)
        shifted = tb[0:1, here] - local
        wb[width : 2 * width, here] = (wb[0:width, here].astype(F32) * shifted).astype(BF16)
        tail = sign8 + three_rows(split3(shifted * sign), 1)
        wb[2 * width : 2 * width + 16, here] = jnp.concatenate([tail, none8], axis=0).astype(BF16)
        return carry

    lax.fori_loop(0, nb, weigh_second, 0)

    def first_sums(ap, carry):
        here = lanes(ap, 2)
        oa[:, here] = matmul_t(wb[...], km[here, :])
        return carry

    first_sums(3, 0)
    for slot in range(1, 16):
        stats(slot).wait_recv()
    every = stat_in[...]
    added = jnp.sum(every, axis=0)
    mean = added[0:1, 0:1] * (1.0 / 16.0)
    away = jnp.sum(jnp.square(every - mean), axis=0)
    spread = added[0:1, 64:65] + float(na * each) * away[0:1, 0:1]
    variance = 4.0 * spread / points**3 + 1e-08
    statistic = mean / points
    deviation = jnp.sqrt(variance)
    coef_a = 1.0 / (points * deviation)
    coef_b = -4.0 * statistic / (points**2 * (variance * deviation))
    objective_ref[...] = jnp.broadcast_to(statistic / deviation, objective_ref.shape)
    base = 2.0 * coef_a + 2.0 * coef_b * (local - mean)
    outer = sign * (-1.0 / width)

    def combine(value, shifted, plain, rho, weighted, tau):
        alpha = base + coef_b * shifted
        return (value * rho - plain) * (alpha * outer) + (value * tau - weighted) * (coef_b * outer)

    def gradient_first(a):
        here = block_lanes(a)
        low = 2 * width
        tau = oa[low + 1 : low + 2, here] + oa[low + 2 : low + 3, here] + oa[low + 3 : low + 4, here]
        return combine(
            at[:, here].astype(F32), ta[0:1, here] - local,
            oa[0:width, here], oa[low : low + 1, here], oa[width:low, here], tau,
        )

    def gradient_second(b):
        here = block_lanes(b)
        tau = o2b[width : width + 1, here] + o2b[width + 1 : width + 2, here] + o2b[width + 2 : width + 3, here]
        return combine(
            bt[0:width, here].astype(F32), tb[0:1, here] - local,
            o1b[0:width, here], o1b[width : width + 1, here], o2b[0:width, here], tau,
        )

    def finish_second(j, carry):
        b = 2 * TWO_SIDED - 1 - j
        gb[:, block_lanes(b)] = gradient_second(b).astype(BF16)
        return_second(b).start()
        return carry

    def finish_first(a):
        ga[:, block_lanes(a)] = gradient_first(a).astype(BF16)
        return_first(a).start()

    def finish_and_sum(j, carry):
        ap = 3 - j
        finish_first(2 * ap)
        finish_first(2 * ap + 1)

        @pl.when(j == 0)
        def _():
            lax.fori_loop(0, 2 * TWO_SIDED, finish_second, 0)

        first_sums(ap - 1, 0)
        return carry

    lax.fori_loop(0, 3, finish_and_sum, 0)
    finish_first(1)
    result = gradient_first(OWN_FIRST)
    for a in first_others:
        return_first(a).wait_recv()
        result = result + g_in[a].astype(F32)
    for b in shared:
        return_second(b).wait_recv()
        result = result + g_in[na + b].astype(F32)
    result = result.T
    grad_pool_ref[...] = result[0:each]
    grad_label_ref[...] = result[each:both]

    for a in first_others:
        for item in (gather_first if a in (1, 2, 4, 6) else forward, partial_first, total_first, return_first):
            item(a).wait_send()
    for b in second_others:
        for item in (gather_second, total_second):
            item(b).wait_send()
    for b in shared:
        for item in (partial_second, return_second):
            item(b).wait_send()
    for slot in range(1, 16):
        stats(slot).wait_send()


def shards(pool, labeled):
    each, width = pool.shape
    both = 2 * each
    deep = width + 16
    na, nb = len(FIRST), len(SECOND)
    la, lb, ls = na * both, nb * both, 2 * TWO_SIDED * both
    dma = pltpu.SemaphoreType.DMA
    vmem = pl.BlockSpec(memory_space=pltpu.VMEM)
    scratch = [
        pltpu.VMEM((both, width), BF16),
        pltpu.VMEM((width, both), BF16),
        pltpu.VMEM((width, la), BF16),
        pltpu.VMEM((2 * width, lb), BF16),
        pltpu.VMEM((la, 2 * width), BF16),
        pltpu.VMEM((la, lb), BF16),
        pltpu.VMEM((la, 128), F32),
        pltpu.VMEM((8, ls + 2 * both), F32),
        pltpu.VMEM((8, both), F32),
        pltpu.VMEM((8, ls), F32),
        pltpu.VMEM((na, 8, both), F32),
        pltpu.VMEM((2 * TWO_SIDED, 8, both), F32),
        pltpu.VMEM((8, both), F32),
        pltpu.VMEM((na, 8, both), F32),
        pltpu.VMEM((8, both), F32),
        pltpu.VMEM((8, la), F32),
        pltpu.VMEM((8, lb), F32),
        pltpu.VMEM((deep, la), BF16),
        pltpu.VMEM((deep, la), BF16),
        pltpu.VMEM((width + deep, lb), BF16),
        pltpu.VMEM((deep, ls), F32),
        pltpu.VMEM((deep, ls), F32),
        pltpu.VMEM((width + deep, la), F32),
        pltpu.VMEM((width, la), BF16),
        pltpu.VMEM((width, ls), BF16),
        pltpu.VMEM((na + nb, width, both), BF16),
        pltpu.VMEM((8, 128), F32),
        pltpu.VMEM((16, 8, 128), F32),
    ]
    for _ in range(4):
        scratch += [dma((na,)), dma((na,)), dma((nb,)), dma((nb,))]
    scratch += [dma((16,)), dma((16,)), dma((2,))]
    grad_pool, grad_label, objective = pl.pallas_call(
        kernel,
        out_shape=(
            jax.ShapeDtypeStruct((each, width), F32),
            jax.ShapeDtypeStruct((each, width), F32),
            jax.ShapeDtypeStruct((8, 128), F32),
        ),
        in_specs=[pl.BlockSpec(memory_space=pl.ANY)] * 2,
        out_specs=(vmem, vmem, vmem),
        scratch_shapes=scratch,
        compiler_params=pltpu.CompilerParams(
            collective_id=0, has_side_effects=True, vmem_limit_bytes=60 * 2**20
        ),
    )(pool, labeled)

    def hand_on(pool_in, label_in, objective_in, pool_out, label_out, objective_out):
        pool_out[...] = pool_in[...]
        label_out[...] = label_in[...]
        objective_out[0, 0] = objective_in[0, 0]

    grad_pool, grad_label, objective = pl.pallas_call(
        hand_on,
        out_shape=(
            jax.ShapeDtypeStruct((each, width), F32),
            jax.ShapeDtypeStruct((each, width), F32),
            jax.ShapeDtypeStruct((1, 1), F32),
        ),
        in_specs=[vmem, vmem, vmem],
        out_specs=(vmem, vmem, pl.BlockSpec(memory_space=pltpu.SMEM)),
    )(grad_pool, grad_label, objective)
    return grad_pool, grad_label, objective.reshape(())


def solution(mesh):
    in_specs = (P(("row", "col"), None), P(("row", "col"), None))
    out_specs = (P(("row", "col"), None), P(("row", "col"), None), P())
    return jax.shard_map(shards, mesh=mesh, in_specs=in_specs, out_specs=out_specs, check_vma=False)
```

```python
import math

import jax
import jax.numpy as jnp
from jax import lax
from jax.experimental import pallas as pl
from jax.experimental.pallas import tpu as pltpu
from jax.sharding import PartitionSpec as P

MESH = pl.DeviceIdType.MESH
F32 = jnp.float32
BF16 = jnp.bfloat16

FIRST = tuple((dx, dk) for dx in range(4) for dk in range(2))
SECOND = ((0, 1), (-1, 0), (1, 1), (-1, 1), (1, 2), (2, -1), (0, 0), (0, 2), (2, 0), (2, 2))
OWN_FIRST = FIRST.index((0, 0))
OWN_SECOND = SECOND.index((0, 0))
RELAY = {
    0: ((0, 1), (0, 1)),
    1: ((-1, 0), (-1, 0)),
    2: ((1, 0), (1, 0)),
    3: ((-1, 0), (0, 1)),
    7: ((0, 1), (0, 1)),
    8: ((-1, 0), (-1, 0)),
    4: ((1, 0), (1, 0)),
    5: ((0, -1), (0, -1)),
    9: ((0, 2), (2, 0)),
}
TWO_SIDED = 3
SECOND_PAIRS = len(SECOND) // 2


def place():
    row, col = lax.axis_index("row"), lax.axis_index("col")
    return ((col // 2) % 2) * 2 + row // 4, col // 4, row % 4, col % 2


def device(x, y, z, core):
    x, y, z, core = (x + 8) % 4, (y + 8) % 4, (z + 8) % 4, (core + 2) % 2
    return ((x % 2) * 4 + z, y * 4 + (x // 2) * 2 + core)


def split3(value):
    high = value.astype(BF16).astype(F32)
    rest = value - high
    middle = rest.astype(BF16).astype(F32)
    return high, middle, rest - middle


def matmul(left, right):
    return lax.dot_general(left, right, (((1,), (0,)), ((), ())), preferred_element_type=F32)


def matmul_t(left, right):
    return lax.dot_general(left, right, (((1,), (1,)), ((), ())), preferred_element_type=F32)


def pick(index, values):
    out = values[-1]
    for i in range(len(values) - 2, -1, -1):
        out = jnp.where(index == i, values[i], out)
    return out


def kernel(
    pool_ref, label_ref, grad_pool_ref, grad_label_ref, objective_ref,
    rows_in, own, at, bt, za, km, acc_a, acc_b, part_a, part_b, first_in, second_in, sum_b, sum_b_in, t_own, ta, tb,
    w1a, w2a, wb, o1b, o2b, oa, ga, gb, g_in, stat_out, stat_in,
    ga_send, ga_recv, gb_send, gb_recv, pa_send, pa_recv, pb_send, pb_recv,
    ta_send, ta_recv, tb_send, tb_recv, ra_send, ra_recv, rb_send, rb_recv, st_send, st_recv, read_sem,
):
    width = pool_ref.shape[1]
    each = pool_ref.shape[0]
    both = 2 * each
    deep = width + 16
    na, nb = len(FIRST), len(SECOND)
    points = float(each * 128)
    x, y, z, core = place()

    def to_first(a):
        return device(x + a // 2, y, z, core + a % 2)

    def from_first(a):
        return device(x - a // 2, y, z, core + a % 2)

    def to_second(b):
        return device(x, y + pick(b, [v[0] for v in SECOND]), z + pick(b, [v[1] for v in SECOND]), core)

    def from_second(b):
        return device(x, y - pick(b, [v[0] for v in SECOND]), z - pick(b, [v[1] for v in SECOND]), core)

    def copy(src, dst, send, recv, target):
        return pltpu.make_async_remote_copy(
            src_ref=src, dst_ref=dst, send_sem=send, recv_sem=recv, device_id=target, device_id_type=MESH
        )

    first_others = [a for a in range(na) if a != OWN_FIRST]
    second_others = [b for b in range(nb) if b != OWN_SECOND]
    shared = range(2 * TWO_SIDED)

    def lanes(index, count=1):
        return pl.ds(pl.multiple_of(index * both * count, both * count), both * count)

    def block_lanes(index):
        return pl.ds(pl.multiple_of(index * both, both), both)

    def gather_first(a):
        return copy(own, at.at[:, block_lanes(a)], ga_send.at[a], ga_recv.at[a], from_first(a))

    def forward(a):
        return copy(
            at.at[:, block_lanes(a - 1)], at.at[:, block_lanes(a)], ga_send.at[a], ga_recv.at[a],
            device(x, y, z, core + 1),
        )

    def gather_second(b):
        if b in (0, 1):
            source = own
        else:
            at_neighbour = {2: 0, 3: jnp.where(core == 0, 0, 1), 4: 7, 5: 8, 7: 0, 8: 1, 9: jnp.where(core == 0, 8, 7)}[b]
            source = bt.at[pl.ds(0, width), block_lanes(at_neighbour)]
        first, other = RELAY[b]
        dy = jnp.where(core == 0, first[0], other[0])
        dz = jnp.where(core == 0, first[1], other[1])
        return copy(
            source, bt.at[pl.ds(0, width), block_lanes(b)], gb_send.at[b], gb_recv.at[b],
            device(x, y - dy, z - dz, core),
        )

    def partial_first(a):
        return copy(part_a, first_in.at[a], pa_send.at[a], pa_recv.at[a], from_first(a))

    def partial_second(b):
        return copy(part_b.at[:, block_lanes(b)], second_in.at[b], pb_send.at[b], pb_recv.at[b], to_second(b))

    def total_first(a):
        return copy(sum_b, sum_b_in.at[a], ta_send.at[a], ta_recv.at[a], from_first(a))

    def total_second(b):
        return copy(t_own, tb.at[:, block_lanes(b)], tb_send.at[b], tb_recv.at[b], from_second(b))

    def return_first(a):
        return copy(ga.at[:, block_lanes(a)], g_in.at[a], ra_send.at[a], ra_recv.at[a], to_first(a))

    def return_second(b):
        return copy(gb.at[:, block_lanes(b)], g_in.at[na + b], rb_send.at[b], rb_recv.at[b], to_second(b))

    def stats(slot):
        target = device(x, y - slot // 4, z - slot % 4, core)
        return copy(stat_out, stat_in.at[slot], st_send.at[slot], st_recv.at[slot], target)

    partners = [(0, 0, 0, 1), (1, 0, 0, 0), (3, 0, 0, 0), (2, 0, 0, 0)]
    partners += [(0, 1, 0, 0), (0, 3, 0, 0), (0, 0, 1, 0), (0, 0, 3, 0)]
    barrier = pltpu.get_barrier_semaphore()
    for dx, dy, dz, dk in partners:
        pl.semaphore_signal(
            barrier, inc=1, device_id=device(x + dx, y + dy, z + dz, core + dk), device_id_type=MESH
        )

    reads = [
        pltpu.make_async_copy(pool_ref, rows_in.at[pl.ds(0, each)], read_sem.at[0]),
        pltpu.make_async_copy(label_ref, rows_in.at[pl.ds(each, each)], read_sem.at[1]),
    ]
    for item in reads:
        item.start()
    sign = jnp.where(lax.broadcasted_iota(jnp.int32, (1, both), 1) < each, 1.0, -1.0).astype(F32)
    for item in reads:
        item.wait()
    rows = rows_in[...].astype(F32)
    block = rows.T.astype(BF16)
    own[...] = block
    at[:, pl.ds(OWN_FIRST * both, both)] = block
    bt[0:width, pl.ds(OWN_SECOND * both, both)] = block
    bt[deep:, :] = jnp.zeros((bt.shape[0] - deep, nb * both), BF16)
    acc_a[...] = jnp.zeros(acc_a.shape, F32)
    acc_b[...] = jnp.zeros(acc_b.shape, F32)

    pl.semaphore_wait(barrier, len(partners))

    for a in (2, 6, 1):
        gather_first(a).start()
    for b in (0, 1):
        gather_second(b).start()
    gather_first(4).start()

    place8 = lax.broadcasted_iota(jnp.int32, (8, both), 0)
    none8 = jnp.zeros((8, both), F32)
    ones8 = jnp.where(place8 < 3, 1.0, none8)
    sign8 = jnp.where(place8 == 0, sign, none8)

    def three_rows(parts, start):
        out = none8
        for i, part in enumerate(parts):
            out = jnp.where(place8 == start + i, part, out)
        return out

    def half_norms(value):
        return three_rows(split3(jnp.sum(value * value, axis=0, keepdims=True) * -0.5), 0)

    def take_first(a):
        here = block_lanes(a)
        value = at[:, here].astype(F32)
        za[here, 0:width] = value.T.astype(BF16)
        rest = jnp.concatenate([ones8, half_norms(value), jnp.zeros((width - 16, both), F32)], axis=0)
        za[here, width : 2 * width] = rest.T.astype(BF16)
        w1a[0:width, here] = (value * sign).astype(BF16)
        w1a[width:deep, here] = jnp.concatenate([sign8, none8], axis=0).astype(BF16)

    def take_second(b):
        here = block_lanes(b)
        value = bt[0:width, here].astype(F32)
        bt[width:deep, here] = jnp.concatenate([half_norms(value), ones8], axis=0).astype(BF16)
        wb[0:width, here] = (value * sign).astype(BF16)

    scale = math.log2(math.e) / width
    tile_sign = sign[:, 128:256]

    def sum_second(w, out):
        def body(pair, carry):
            here = lanes(pair, 2)
            out[:, here] = matmul(w[...], km[:, here])
            return carry

        lax.fori_loop(0, TWO_SIDED, body, 0)

    def turn(expected, following):
        for b in expected:
            gather_second(b).wait_recv()
        for b in following:
            gather_second(b).start()

    def once(t, steps, action):
        chosen = t == steps[0]
        for step in steps[1:]:
            chosen = chosen | (t == step)
        pl.when(chosen)(action)

    def kernel_step(t, carry):
        late = t - 8
        pair = jnp.where(t < 3, 0, jnp.where(t < 6, 1, jnp.where(t < 8, t - 6, pick(late // 4, (3, 2, 4)))))
        ap = jnp.where(t < 6, pick(t % 3, (0, 1, 3)), jnp.where(t < 8, 2, late % 4))

        def relay_first(a):
            gather_first(a).wait_recv()
            forward(a + 1).start()

        once(t, (0,), lambda: turn((0, 1), (2, 3, 7, 8)))
        once(t, (3,), lambda: turn((2, 3, 7, 8), (4, 5, 9)))
        once(t, (12,), lambda: turn((4, 5), ()))
        once(t, (16,), lambda: turn((9,), ()))
        once(t, (0,), lambda: relay_first(2))
        once(t, (1,), lambda: relay_first(6))
        once(t, (4,), lambda: relay_first(4))

        def new_second():
            take_second(2 * pair)
            take_second(2 * pair + 1)

        def new_first():
            gather_first(2 * ap + 1).wait_recv()
            take_first(2 * ap)
            take_first(2 * ap + 1)

        once(t, (0, 3, 8, 12, 16), new_second)
        once(t, (0, 1, 2, 6), new_first)
        wide = lanes(pair, 2)
        here = lanes(ap, 2)
        product = matmul(za[here, :], bt[:, wide])
        value = jnp.exp2(product * scale)
        km[here, wide] = value.astype(BF16)
        tiles = [value[:, 128 * j : 128 * (j + 1)] for j in range(6)]
        across = (tiles[0] - tiles[2]) + (tiles[3] - tiles[5]) + (tiles[1] + tiles[4]) * tile_sign
        acc_a[here, :] += across
        parts = [
            jnp.sum(value[each * j : each * (j + 1)].reshape(each // 8, 8, 2 * both), axis=0) for j in range(4)
        ]
        acc_b[:, lanes(jnp.minimum(pair, TWO_SIDED), 2)] += (parts[0] - parts[1]) + (parts[2] - parts[3])

        def second_done():
            for b in (2 * pair, 2 * pair + 1):
                here = block_lanes(b)
                total = jnp.sum(acc_b[:, here], axis=0, keepdims=True) * sign
                part_b[:, here] = total
                partial_second(b).start()

        once(t, (6, 7, 15), second_done)
        return carry

    lax.fori_loop(0, 4 * SECOND_PAIRS, kernel_step, 0)

    rows8 = none8
    for a in range(na):
        rows8 = jnp.where(place8 == a, jnp.sum(acc_a[a * both : (a + 1) * both, :].T, axis=0, keepdims=True), rows8)
    part_a[...] = rows8 * sign
    for a in first_others:
        partial_first(a).start()
    got = jnp.zeros((1, both), F32)
    for b in shared:
        partial_second(b).wait_recv()
        got = got + second_in[b]
    sum_b[...] = got
    for a in first_others:
        total_first(a).start()
    sum_second(w1a, o1b)

    def seen_from(value, a):
        dx, dk = FIRST[a]
        if dk:
            value = jnp.where(place8 % 2 == 0, pltpu.roll(value, 7, 0), pltpu.roll(value, 1, 0))
        return pltpu.roll(value, 2 * dx, 0) if dx else value

    total = part_a[...]
    for a in first_others:
        partial_first(a).wait_recv()
        total = total + seen_from(first_in[a], a)
    total = total + jnp.where(place8 == OWN_FIRST, got, 0.0)
    for a in first_others:
        total_first(a).wait_recv()
        total = total + jnp.where(place8 == a, sum_b_in[a], 0.0)
    total = total + pltpu.roll(total, each, 1)
    for a in range(na):
        ta[:, a * both : (a + 1) * both] = jnp.broadcast_to(total[a : a + 1], (8, both))
    mine = total[OWN_FIRST : OWN_FIRST + 1]
    t_own[...] = mine
    tb[:, pl.ds(OWN_SECOND * both, both)] = mine
    for b in (9, 4, 5, 8, 7, 3, 2, 1, 0):
        total_second(b).start()

    line = ta[0:1, :]
    local = jnp.sum(line, axis=1, keepdims=True) / (na * both)
    spread = 0.5 * jnp.sum(jnp.square(line - local), axis=1, keepdims=True)
    told = jnp.where(lax.broadcasted_iota(jnp.int32, (1, 128), 1) < 64, local, spread)
    stat_out[...] = told
    stat_in[0] = told
    for slot in range(1, 16):
        stats(slot).start()

    def weigh_first(a, carry):
        here = block_lanes(a)
        shifted = ta[0:1, here] - local
        w2a[0:width, here] = (w1a[0:width, here].astype(F32) * shifted).astype(BF16)
        w2a[width:deep, here] = jnp.concatenate([three_rows(split3(shifted * sign), 0), none8], axis=0).astype(BF16)
        return carry

    lax.fori_loop(0, na, weigh_first, 0)

    sum_second(w2a, o2b)
    for b in second_others:
        total_second(b).wait_recv()

    def weigh_second(b, carry):
        here = block_lanes(b)
        shifted = tb[0:1, here] - local
        wb[width : 2 * width, here] = (wb[0:width, here].astype(F32) * shifted).astype(BF16)
        tail = sign8 + three_rows(split3(shifted * sign), 1)
        wb[2 * width : 2 * width + 16, here] = jnp.concatenate([tail, none8], axis=0).astype(BF16)
        return carry

    lax.fori_loop(0, nb, weigh_second, 0)

    def first_sums(ap, carry):
        here = lanes(ap, 2)
        oa[:, here] = matmul_t(wb[...], km[here, :])
        return carry

    first_sums(2, 0)
    for slot in range(1, 16):
        stats(slot).wait_recv()
    every = stat_in[...]
    added = jnp.sum(every, axis=0)
    mean = added[0:1, 0:1] * (1.0 / 16.0)
    away = jnp.sum(jnp.square(every - mean), axis=0)
    spread = added[0:1, 64:65] + float(na * each) * away[0:1, 0:1]
    variance = 4.0 * spread / points**3 + 1e-08
    statistic = mean / points
    deviation = jnp.sqrt(variance)
    coef_a = 1.0 / (points * deviation)
    coef_b = -4.0 * statistic / (points**2 * (variance * deviation))
    objective_ref[...] = jnp.broadcast_to(statistic / deviation, objective_ref.shape)
    base = 2.0 * coef_a + 2.0 * coef_b * (local - mean)
    outer = sign * (-1.0 / width)

    def combine(value, shifted, plain, rho, weighted, tau):
        alpha = base + coef_b * shifted
        return (value * rho - plain) * (alpha * outer) + (value * tau - weighted) * (coef_b * outer)

    def gradient_first(a):
        here = block_lanes(a)
        low = 2 * width
        tau = oa[low + 1 : low + 2, here] + oa[low + 2 : low + 3, here] + oa[low + 3 : low + 4, here]
        return combine(
            at[:, here].astype(F32), ta[0:1, here] - local,
            oa[0:width, here], oa[low : low + 1, here], oa[width:low, here], tau,
        )

    def gradient_second(b):
        here = block_lanes(b)
        tau = o2b[width : width + 1, here] + o2b[width + 1 : width + 2, here] + o2b[width + 2 : width + 3, here]
        return combine(
            bt[0:width, here].astype(F32), tb[0:1, here] - local,
            o1b[0:width, here], o1b[width : width + 1, here], o2b[0:width, here], tau,
        )

    def finish_second(j, carry):
        b = 2 * TWO_SIDED - 1 - j
        gb[:, block_lanes(b)] = gradient_second(b).astype(BF16)
        return_second(b).start()
        return carry

    def finish_first(a):
        ga[:, block_lanes(a)] = gradient_first(a).astype(BF16)
        return_first(a).start()

    def finish_and_sum(j, carry):
        ap = pick(j, (2, 3, 1))
        finish_first(2 * ap)
        finish_first(2 * ap + 1)

        @pl.when(j == 0)
        def _():
            lax.fori_loop(0, 2 * TWO_SIDED, finish_second, 0)

        first_sums(pick(j, (3, 1, 0)), 0)
        return carry

    lax.fori_loop(0, 3, finish_and_sum, 0)
    finish_first(1)
    result = gradient_first(OWN_FIRST)
    for b in shared:
        return_second(b).wait_recv()
        result = result + g_in[na + b].astype(F32)
    for a in (1, 4, 5, 6, 7, 2, 3):
        return_first(a).wait_recv()
        result = result + g_in[a].astype(F32)
    result = result.T
    grad_pool_ref[...] = result[0:each]
    grad_label_ref[...] = result[each:both]

    for a in first_others:
        for item in (gather_first if a in (1, 2, 4, 6) else forward, partial_first, total_first, return_first):
            item(a).wait_send()
    for b in second_others:
        for item in (gather_second, total_second):
            item(b).wait_send()
    for b in shared:
        for item in (partial_second, return_second):
            item(b).wait_send()
    for slot in range(1, 16):
        stats(slot).wait_send()


def shards(pool, labeled):
    each, width = pool.shape
    both = 2 * each
    deep = width + 16
    na, nb = len(FIRST), len(SECOND)
    la, lb, ls = na * both, nb * both, 2 * TWO_SIDED * both
    dma = pltpu.SemaphoreType.DMA
    vmem = pl.BlockSpec(memory_space=pltpu.VMEM)
    scratch = [
        pltpu.VMEM((both, width), BF16),
        pltpu.VMEM((width, both), BF16),
        pltpu.VMEM((width, la), BF16),
        pltpu.VMEM((2 * width, lb), BF16),
        pltpu.VMEM((la, 2 * width), BF16),
        pltpu.VMEM((la, lb), BF16),
        pltpu.VMEM((la, 128), F32),
        pltpu.VMEM((8, ls + 2 * both), F32),
        pltpu.VMEM((8, both), F32),
        pltpu.VMEM((1, ls), F32),
        pltpu.VMEM((na, 8, both), F32),
        pltpu.VMEM((2 * TWO_SIDED, 1, both), F32),
        pltpu.VMEM((1, both), F32),
        pltpu.VMEM((na, 1, both), F32),
        pltpu.VMEM((1, both), F32),
        pltpu.VMEM((8, la), F32),
        pltpu.VMEM((1, lb), F32),
        pltpu.VMEM((deep, la), BF16),
        pltpu.VMEM((deep, la), BF16),
        pltpu.VMEM((width + deep, lb), BF16),
        pltpu.VMEM((deep, ls), F32),
        pltpu.VMEM((deep, ls), F32),
        pltpu.VMEM((width + deep, la), F32),
        pltpu.VMEM((width, la), BF16),
        pltpu.VMEM((width, ls), BF16),
        pltpu.VMEM((na + nb, width, both), BF16),
        pltpu.VMEM((1, 128), F32),
        pltpu.VMEM((16, 1, 128), F32),
    ]
    for _ in range(4):
        scratch += [dma((na,)), dma((na,)), dma((nb,)), dma((nb,))]
    scratch += [dma((16,)), dma((16,)), dma((2,))]
    grad_pool, grad_label, objective = pl.pallas_call(
        kernel,
        out_shape=(
            jax.ShapeDtypeStruct((each, width), F32),
            jax.ShapeDtypeStruct((each, width), F32),
            jax.ShapeDtypeStruct((8, 128), F32),
        ),
        in_specs=[pl.BlockSpec(memory_space=pl.ANY)] * 2,
        out_specs=(vmem, vmem, vmem),
        scratch_shapes=scratch,
        compiler_params=pltpu.CompilerParams(
            collective_id=0, has_side_effects=True, vmem_limit_bytes=60 * 2**20
        ),
    )(pool, labeled)

    def hand_on(pool_in, label_in, objective_in, pool_out, label_out, objective_out):
        pool_out[...] = pool_in[...]
        label_out[...] = label_in[...]
        objective_out[0, 0] = objective_in[0, 0]

    grad_pool, grad_label, objective = pl.pallas_call(
        hand_on,
        out_shape=(
            jax.ShapeDtypeStruct((each, width), F32),
            jax.ShapeDtypeStruct((each, width), F32),
            jax.ShapeDtypeStruct((1, 1), F32),
        ),
        in_specs=[vmem, vmem, vmem],
        out_specs=(vmem, vmem, pl.BlockSpec(memory_space=pltpu.SMEM)),
    )(grad_pool, grad_label, objective)
    return grad_pool, grad_label, objective.reshape(())


def solution(mesh):
    in_specs = (P(("row", "col"), None), P(("row", "col"), None))
    out_specs = (P(("row", "col"), None), P(("row", "col"), None), P())
    return jax.shard_map(shards, mesh=mesh, in_specs=in_specs, out_specs=out_specs, check_vma=False)
```

```python
import math

import jax
import jax.numpy as jnp
from jax import lax
from jax.experimental import pallas as pl
from jax.experimental.pallas import tpu as pltpu
from jax.sharding import PartitionSpec as P

MESH = pl.DeviceIdType.MESH
F32 = jnp.float32
BF16 = jnp.bfloat16

FIRST = tuple((dx, dk) for dx in range(4) for dk in range(2))
SECOND = ((0, 1), (-1, 0), (1, 1), (-1, 1), (1, 2), (2, -1), (0, 0), (0, 2), (2, 0), (2, 2))
OWN_FIRST = FIRST.index((0, 0))
OWN_SECOND = SECOND.index((0, 0))
RELAY = {
    0: ((0, 1), (0, 1)),
    1: ((-1, 0), (-1, 0)),
    2: ((1, 0), (1, 0)),
    3: ((-1, 0), (0, 1)),
    7: ((0, 1), (0, 1)),
    8: ((-1, 0), (-1, 0)),
    4: ((1, 0), (1, 0)),
    5: ((0, -1), (0, -1)),
    9: ((0, 2), (2, 0)),
}
TWO_SIDED = 3
SECOND_PAIRS = len(SECOND) // 2


def place():
    row, col = lax.axis_index("row"), lax.axis_index("col")
    return ((col // 2) % 2) * 2 + row // 4, col // 4, row % 4, col % 2


def device(x, y, z, core):
    x, y, z, core = (x + 8) % 4, (y + 8) % 4, (z + 8) % 4, (core + 2) % 2
    return ((x % 2) * 4 + z, y * 4 + (x // 2) * 2 + core)


def split3(value):
    high = value.astype(BF16).astype(F32)
    rest = value - high
    middle = rest.astype(BF16).astype(F32)
    return high, middle, rest - middle


def matmul(left, right):
    return lax.dot_general(left, right, (((1,), (0,)), ((), ())), preferred_element_type=F32)


def matmul_t(left, right):
    return lax.dot_general(left, right, (((1,), (1,)), ((), ())), preferred_element_type=F32)


def pick(index, values):
    out = values[-1]
    for i in range(len(values) - 2, -1, -1):
        out = jnp.where(index == i, values[i], out)
    return out


def kernel(
    pool_ref, label_ref, grad_pool_ref, grad_label_ref, objective_ref,
    rows_in, own, at, bt, za, km, acc_a, acc_b, part_a, part_b, first_in, second_in, sum_b, sum_b_in, t_own, ta, tb,
    w1a, w2a, wb, o1b, o2b, oa, ga, gb, g_in, stat_out, stat_in,
    ga_send, ga_recv, gb_send, gb_recv, pa_send, pa_recv, pb_send, pb_recv,
    ta_send, ta_recv, tb_send, tb_recv, ra_send, ra_recv, rb_send, rb_recv, st_send, st_recv, read_sem,
):
    width = pool_ref.shape[1]
    each = pool_ref.shape[0]
    both = 2 * each
    deep = width + 16
    na, nb = len(FIRST), len(SECOND)
    points = float(each * 128)
    x, y, z, core = place()

    def to_first(a):
        return device(x + a // 2, y, z, core + a % 2)

    def from_first(a):
        return device(x - a // 2, y, z, core + a % 2)

    def to_second(b):
        return device(x, y + pick(b, [v[0] for v in SECOND]), z + pick(b, [v[1] for v in SECOND]), core)

    def from_second(b):
        return device(x, y - pick(b, [v[0] for v in SECOND]), z - pick(b, [v[1] for v in SECOND]), core)

    def copy(src, dst, send, recv, target):
        return pltpu.make_async_remote_copy(
            src_ref=src, dst_ref=dst, send_sem=send, recv_sem=recv, device_id=target, device_id_type=MESH
        )

    first_others = [a for a in range(na) if a != OWN_FIRST]
    second_others = [b for b in range(nb) if b != OWN_SECOND]
    shared = range(2 * TWO_SIDED)

    def lanes(index, count=1):
        return pl.ds(pl.multiple_of(index * both * count, both * count), both * count)

    def block_lanes(index):
        return pl.ds(pl.multiple_of(index * both, both), both)

    def gather_first(a):
        return copy(own, at.at[:, block_lanes(a)], ga_send.at[a], ga_recv.at[a], from_first(a))

    def forward(a):
        return copy(
            at.at[:, block_lanes(a - 1)], at.at[:, block_lanes(a)], ga_send.at[a], ga_recv.at[a],
            device(x, y, z, core + 1),
        )

    def gather_second(b):
        if b in (0, 1):
            source = own
        else:
            at_neighbour = {2: 0, 3: jnp.where(core == 0, 0, 1), 4: 7, 5: 8, 7: 0, 8: 1, 9: jnp.where(core == 0, 8, 7)}[b]
            source = bt.at[pl.ds(0, width), block_lanes(at_neighbour)]
        first, other = RELAY[b]
        dy = jnp.where(core == 0, first[0], other[0])
        dz = jnp.where(core == 0, first[1], other[1])
        return copy(
            source, bt.at[pl.ds(0, width), block_lanes(b)], gb_send.at[b], gb_recv.at[b],
            device(x, y - dy, z - dz, core),
        )

    def partial_first(a):
        return copy(part_a, first_in.at[a], pa_send.at[a], pa_recv.at[a], from_first(a))

    def partial_second(b):
        return copy(part_b.at[:, block_lanes(b)], second_in.at[b], pb_send.at[b], pb_recv.at[b], to_second(b))

    def total_first(a):
        return copy(sum_b, sum_b_in.at[a], ta_send.at[a], ta_recv.at[a], from_first(a))

    def total_second(b):
        return copy(t_own, tb.at[:, block_lanes(b)], tb_send.at[b], tb_recv.at[b], from_second(b))

    def return_first(a):
        return copy(ga.at[:, block_lanes(a)], g_in.at[a], ra_send.at[a], ra_recv.at[a], to_first(a))

    def return_second(b):
        return copy(gb.at[:, block_lanes(b)], g_in.at[na + b], rb_send.at[b], rb_recv.at[b], to_second(b))

    def stats(slot):
        target = device(x, y - slot // 4, z - slot % 4, core)
        return copy(stat_out, stat_in.at[slot], st_send.at[slot], st_recv.at[slot], target)

    partners = [(0, 0, 0, 1), (1, 0, 0, 0), (3, 0, 0, 0), (2, 0, 0, 0)]
    partners += [(0, 1, 0, 0), (0, 3, 0, 0), (0, 0, 1, 0), (0, 0, 3, 0)]
    barrier = pltpu.get_barrier_semaphore()
    for dx, dy, dz, dk in partners:
        pl.semaphore_signal(
            barrier, inc=1, device_id=device(x + dx, y + dy, z + dz, core + dk), device_id_type=MESH
        )

    reads = [
        pltpu.make_async_copy(pool_ref, rows_in.at[pl.ds(0, each)], read_sem.at[0]),
        pltpu.make_async_copy(label_ref, rows_in.at[pl.ds(each, each)], read_sem.at[1]),
    ]
    for item in reads:
        item.start()
    sign = jnp.where(lax.broadcasted_iota(jnp.int32, (1, both), 1) < each, 1.0, -1.0).astype(F32)
    for item in reads:
        item.wait()
    rows = rows_in[...].astype(F32)
    block = rows.T.astype(BF16)
    own[...] = block
    at[:, pl.ds(OWN_FIRST * both, both)] = block
    bt[0:width, pl.ds(OWN_SECOND * both, both)] = block
    bt[deep:, :] = jnp.zeros((bt.shape[0] - deep, nb * both), BF16)
    acc_a[...] = jnp.zeros(acc_a.shape, F32)
    acc_b[...] = jnp.zeros(acc_b.shape, F32)

    pl.semaphore_wait(barrier, len(partners))

    for a in (2, 6, 1):
        gather_first(a).start()
    for b in (0, 1):
        gather_second(b).start()
    gather_first(4).start()

    place8 = lax.broadcasted_iota(jnp.int32, (8, both), 0)
    none8 = jnp.zeros((8, both), F32)
    ones8 = jnp.where(place8 < 3, 1.0, none8)
    sign8 = jnp.where(place8 == 0, sign, none8)

    def three_rows(parts, start):
        out = none8
        for i, part in enumerate(parts):
            out = jnp.where(place8 == start + i, part, out)
        return out

    def half_norms(value):
        return three_rows(split3(jnp.sum(value * value, axis=0, keepdims=True) * -0.5), 0)

    def take_first(a):
        here = block_lanes(a)
        value = at[:, here].astype(F32)
        za[here, 0:width] = value.T.astype(BF16)
        rest = jnp.concatenate([ones8, half_norms(value), jnp.zeros((width - 16, both), F32)], axis=0)
        za[here, width : 2 * width] = rest.T.astype(BF16)
        w1a[0:width, here] = (value * sign).astype(BF16)
        w1a[width:deep, here] = jnp.concatenate([sign8, none8], axis=0).astype(BF16)

    def take_second(b):
        here = block_lanes(b)
        value = bt[0:width, here].astype(F32)
        bt[width:deep, here] = jnp.concatenate([half_norms(value), ones8], axis=0).astype(BF16)
        wb[0:width, here] = (value * sign).astype(BF16)

    scale = math.log2(math.e) / width
    tile_sign = sign[:, 128:256]

    def sum_second(w, out):
        def body(pair, carry):
            here = lanes(pair, 2)
            out[:, here] = matmul(w[...], km[:, here])
            return carry

        lax.fori_loop(0, TWO_SIDED, body, 0)

    def turn(expected, following):
        for b in expected:
            gather_second(b).wait_recv()
        for b in following:
            gather_second(b).start()

    def once(t, steps, action):
        chosen = t == steps[0]
        for step in steps[1:]:
            chosen = chosen | (t == step)
        pl.when(chosen)(action)

    def form(pair, place, count):
        wide = lanes(pair, 2)
        here = lanes(place, 2 * count)
        product = matmul(za[here, :], bt[:, wide])
        value = jnp.exp2(product * scale)
        km[here, wide] = value.astype(BF16)
        tiles = [value[:, 128 * j : 128 * (j + 1)] for j in range(6)]
        across = (tiles[0] - tiles[2]) + (tiles[3] - tiles[5]) + (tiles[1] + tiles[4]) * tile_sign
        acc_a[here, :] += across
        parts = [
            jnp.sum(value[each * j : each * (j + 1)].reshape(each // 8, 8, 2 * both), axis=0) for j in range(4 * count)
        ]
        down = sum(parts[2::2], parts[0]) - sum(parts[3::2], parts[1])
        acc_b[:, lanes(jnp.minimum(pair, TWO_SIDED), 2)] += down

    def new_second(pair):
        take_second(2 * pair)
        take_second(2 * pair + 1)

    def second_done(pair):
        for b in (2 * pair, 2 * pair + 1):
            here = block_lanes(b)
            part_b[:, here] = jnp.sum(acc_b[:, here], axis=0, keepdims=True) * sign
            partial_second(b).start()

    def early_step(t, carry):
        pair = jnp.where(t < 6, t // 3, t - 6)
        ap = jnp.where(t < 6, pick(t % 3, (0, 1, 3)), 2)

        def relay_first(a):
            gather_first(a).wait_recv()
            forward(a + 1).start()

        once(t, (0,), lambda: turn((0, 1), (2, 3, 7, 8)))
        once(t, (3,), lambda: turn((2, 3, 7, 8), (4, 5, 9)))
        once(t, (0,), lambda: relay_first(2))
        once(t, (1,), lambda: relay_first(6))
        once(t, (4,), lambda: relay_first(4))

        def new_first():
            gather_first(2 * ap + 1).wait_recv()
            take_first(2 * ap)
            take_first(2 * ap + 1)

        once(t, (0, 3), lambda: new_second(pair))
        once(t, (0, 1, 2, 6), new_first)
        form(pair, ap, 1)
        once(t, (6, 7), lambda: second_done(pair))
        return carry

    def late_step(t, carry):
        pair = pick(t // 2, (3, 2, 4))
        once(t, (2,), lambda: turn((4, 5), ()))
        once(t, (4,), lambda: turn((9,), ()))
        once(t, (0, 2, 4), lambda: new_second(pair))
        form(pair, t % 2, 2)
        once(t, (3,), lambda: second_done(pair))
        return carry

    lax.fori_loop(0, 8, early_step, 0)
    lax.fori_loop(0, 6, late_step, 0)

    rows8 = none8
    for a in range(na):
        rows8 = jnp.where(place8 == a, jnp.sum(acc_a[a * both : (a + 1) * both, :].T, axis=0, keepdims=True), rows8)
    part_a[...] = rows8 * sign
    for a in first_others:
        partial_first(a).start()
    got = jnp.zeros((1, both), F32)
    for b in shared:
        partial_second(b).wait_recv()
        got = got + second_in[b]
    sum_b[...] = got
    for a in first_others:
        total_first(a).start()
    sum_second(w1a, o1b)

    def seen_from(value, a):
        dx, dk = FIRST[a]
        if dk:
            value = jnp.where(place8 % 2 == 0, pltpu.roll(value, 7, 0), pltpu.roll(value, 1, 0))
        return pltpu.roll(value, 2 * dx, 0) if dx else value

    total = part_a[...]
    for a in first_others:
        partial_first(a).wait_recv()
        total = total + seen_from(first_in[a], a)
    total = total + jnp.where(place8 == OWN_FIRST, got, 0.0)
    for a in first_others:
        total_first(a).wait_recv()
        total = total + jnp.where(place8 == a, sum_b_in[a], 0.0)
    total = total + pltpu.roll(total, each, 1)
    for a in range(na):
        ta[:, a * both : (a + 1) * both] = jnp.broadcast_to(total[a : a + 1], (8, both))
    mine = total[OWN_FIRST : OWN_FIRST + 1]
    t_own[...] = mine
    tb[:, pl.ds(OWN_SECOND * both, both)] = mine
    for b in (9, 4, 5, 8, 7, 3, 2, 1, 0):
        total_second(b).start()

    line = ta[0:1, :]
    local = jnp.sum(line, axis=1, keepdims=True) / (na * both)
    spread = 0.5 * jnp.sum(jnp.square(line - local), axis=1, keepdims=True)
    told = jnp.where(lax.broadcasted_iota(jnp.int32, (1, 128), 1) < 64, local, spread)
    stat_out[...] = told
    stat_in[0] = told
    for slot in range(1, 16):
        stats(slot).start()

    def weigh_first(a, carry):
        here = block_lanes(a)
        shifted = ta[0:1, here] - local
        w2a[0:width, here] = (w1a[0:width, here].astype(F32) * shifted).astype(BF16)
        w2a[width:deep, here] = jnp.concatenate([three_rows(split3(shifted * sign), 0), none8], axis=0).astype(BF16)
        return carry

    lax.fori_loop(0, na, weigh_first, 0)

    sum_second(w2a, o2b)
    for b in second_others:
        total_second(b).wait_recv()

    def weigh_second(b, carry):
        here = block_lanes(b)
        shifted = tb[0:1, here] - local
        wb[width : 2 * width, here] = (wb[0:width, here].astype(F32) * shifted).astype(BF16)
        tail = sign8 + three_rows(split3(shifted * sign), 1)
        wb[2 * width : 2 * width + 16, here] = jnp.concatenate([tail, none8], axis=0).astype(BF16)
        return carry

    lax.fori_loop(0, nb, weigh_second, 0)

    def first_sums(ap, carry):
        here = lanes(ap, 2)
        oa[:, here] = matmul_t(wb[...], km[here, :])
        return carry

    first_sums(2, 0)
    for slot in range(1, 16):
        stats(slot).wait_recv()
    every = stat_in[...]
    added = jnp.sum(every, axis=0)
    mean = added[0:1, 0:1] * (1.0 / 16.0)
    away = jnp.sum(jnp.square(every - mean), axis=0)
    spread = added[0:1, 64:65] + float(na * each) * away[0:1, 0:1]
    variance = 4.0 * spread / points**3 + 1e-08
    statistic = mean / points
    deviation = jnp.sqrt(variance)
    coef_a = 1.0 / (points * deviation)
    coef_b = -4.0 * statistic / (points**2 * (variance * deviation))
    objective_ref[...] = jnp.broadcast_to(statistic / deviation, objective_ref.shape)
    base = 2.0 * coef_a + 2.0 * coef_b * (local - mean)
    outer = sign * (-1.0 / width)

    def combine(value, shifted, plain, rho, weighted, tau):
        alpha = base + coef_b * shifted
        return (value * rho - plain) * (alpha * outer) + (value * tau - weighted) * (coef_b * outer)

    def gradient_first(a):
        here = block_lanes(a)
        low = 2 * width
        tau = oa[low + 1 : low + 2, here] + oa[low + 2 : low + 3, here] + oa[low + 3 : low + 4, here]
        return combine(
            at[:, here].astype(F32), ta[0:1, here] - local,
            oa[0:width, here], oa[low : low + 1, here], oa[width:low, here], tau,
        )

    def gradient_second(b):
        here = block_lanes(b)
        tau = o2b[width : width + 1, here] + o2b[width + 1 : width + 2, here] + o2b[width + 2 : width + 3, here]
        return combine(
            bt[0:width, here].astype(F32), tb[0:1, here] - local,
            o1b[0:width, here], o1b[width : width + 1, here], o2b[0:width, here], tau,
        )

    def finish_second(j, carry):
        b = 2 * TWO_SIDED - 1 - j
        gb[:, block_lanes(b)] = gradient_second(b).astype(BF16)
        return_second(b).start()
        return carry

    def finish_first(a):
        ga[:, block_lanes(a)] = gradient_first(a).astype(BF16)
        return_first(a).start()

    def finish_and_sum(j, carry):
        ap = pick(j, (2, 3, 1))
        finish_first(2 * ap)
        finish_first(2 * ap + 1)

        @pl.when(j == 0)
        def _():
            lax.fori_loop(0, 2 * TWO_SIDED, finish_second, 0)

        first_sums(pick(j, (3, 1, 0)), 0)
        return carry

    lax.fori_loop(0, 3, finish_and_sum, 0)
    finish_first(1)
    result = gradient_first(OWN_FIRST)
    for b in shared:
        return_second(b).wait_recv()
        result = result + g_in[na + b].astype(F32)
    for a in (1, 4, 5, 6, 7, 2, 3):
        return_first(a).wait_recv()
        result = result + g_in[a].astype(F32)
    result = result.T
    grad_pool_ref[...] = result[0:each]
    grad_label_ref[...] = result[each:both]

    for a in first_others:
        for item in (gather_first if a in (1, 2, 4, 6) else forward, partial_first, total_first, return_first):
            item(a).wait_send()
    for b in second_others:
        for item in (gather_second, total_second):
            item(b).wait_send()
    for b in shared:
        for item in (partial_second, return_second):
            item(b).wait_send()
    for slot in range(1, 16):
        stats(slot).wait_send()


def shards(pool, labeled):
    each, width = pool.shape
    both = 2 * each
    deep = width + 16
    na, nb = len(FIRST), len(SECOND)
    la, lb, ls = na * both, nb * both, 2 * TWO_SIDED * both
    dma = pltpu.SemaphoreType.DMA
    vmem = pl.BlockSpec(memory_space=pltpu.VMEM)
    scratch = [
        pltpu.VMEM((both, width), BF16),
        pltpu.VMEM((width, both), BF16),
        pltpu.VMEM((width, la), BF16),
        pltpu.VMEM((2 * width, lb), BF16),
        pltpu.VMEM((la, 2 * width), BF16),
        pltpu.VMEM((la, lb), BF16),
        pltpu.VMEM((la, 128), F32),
        pltpu.VMEM((8, ls + 2 * both), F32),
        pltpu.VMEM((8, both), F32),
        pltpu.VMEM((1, ls), F32),
        pltpu.VMEM((na, 8, both), F32),
        pltpu.VMEM((2 * TWO_SIDED, 1, both), F32),
        pltpu.VMEM((1, both), F32),
        pltpu.VMEM((na, 1, both), F32),
        pltpu.VMEM((1, both), F32),
        pltpu.VMEM((8, la), F32),
        pltpu.VMEM((1, lb), F32),
        pltpu.VMEM((deep, la), BF16),
        pltpu.VMEM((deep, la), BF16),
        pltpu.VMEM((width + deep, lb), BF16),
        pltpu.VMEM((deep, ls), F32),
        pltpu.VMEM((deep, ls), F32),
        pltpu.VMEM((width + deep, la), F32),
        pltpu.VMEM((width, la), BF16),
        pltpu.VMEM((width, ls), BF16),
        pltpu.VMEM((na + nb, width, both), BF16),
        pltpu.VMEM((1, 128), F32),
        pltpu.VMEM((16, 1, 128), F32),
    ]
    for _ in range(4):
        scratch += [dma((na,)), dma((na,)), dma((nb,)), dma((nb,))]
    scratch += [dma((16,)), dma((16,)), dma((2,))]
    grad_pool, grad_label, objective = pl.pallas_call(
        kernel,
        out_shape=(
            jax.ShapeDtypeStruct((each, width), F32),
            jax.ShapeDtypeStruct((each, width), F32),
            jax.ShapeDtypeStruct((8, 128), F32),
        ),
        in_specs=[pl.BlockSpec(memory_space=pl.ANY)] * 2,
        out_specs=(vmem, vmem, vmem),
        scratch_shapes=scratch,
        compiler_params=pltpu.CompilerParams(
            collective_id=0, has_side_effects=True, vmem_limit_bytes=60 * 2**20
        ),
    )(pool, labeled)

    def hand_on(pool_in, label_in, objective_in, pool_out, label_out, objective_out):
        pool_out[...] = pool_in[...]
        label_out[...] = label_in[...]
        objective_out[0, 0] = objective_in[0, 0]

    grad_pool, grad_label, objective = pl.pallas_call(
        hand_on,
        out_shape=(
            jax.ShapeDtypeStruct((each, width), F32),
            jax.ShapeDtypeStruct((each, width), F32),
            jax.ShapeDtypeStruct((1, 1), F32),
        ),
        in_specs=[vmem, vmem, vmem],
        out_specs=(vmem, vmem, pl.BlockSpec(memory_space=pltpu.SMEM)),
    )(grad_pool, grad_label, objective)
    return grad_pool, grad_label, objective.reshape(())


def solution(mesh):
    in_specs = (P(("row", "col"), None), P(("row", "col"), None))
    out_specs = (P(("row", "col"), None), P(("row", "col"), None), P())
    return jax.shard_map(shards, mesh=mesh, in_specs=in_specs, out_specs=out_specs, check_vma=False)
```

```python
import math

import jax
import jax.numpy as jnp
from jax import lax
from jax.experimental import pallas as pl
from jax.experimental.pallas import tpu as pltpu
from jax.sharding import PartitionSpec as P

MESH = pl.DeviceIdType.MESH
F32 = jnp.float32
BF16 = jnp.bfloat16

FIRST = tuple((dx, dk) for dx in range(4) for dk in range(2))
SECOND = ((0, 1), (-1, 0), (1, 1), (-1, 1), (1, 2), (2, -1), (0, 0), (0, 2), (2, 0), (2, 2))
OWN_FIRST = FIRST.index((0, 0))
OWN_SECOND = SECOND.index((0, 0))
RELAY = {
    0: ((0, 1), (0, 1)),
    1: ((-1, 0), (-1, 0)),
    2: ((1, 0), (1, 0)),
    3: ((-1, 0), (0, 1)),
    7: ((0, 1), (0, 1)),
    8: ((-1, 0), (-1, 0)),
    4: ((1, 0), (1, 0)),
    5: ((0, -1), (0, -1)),
    9: ((0, 2), (2, 0)),
}
TWO_SIDED = 3
SECOND_PAIRS = len(SECOND) // 2


def place():
    row, col = lax.axis_index("row"), lax.axis_index("col")
    return ((col // 2) % 2) * 2 + row // 4, col // 4, row % 4, col % 2


def device(x, y, z, core):
    x, y, z, core = (x + 8) % 4, (y + 8) % 4, (z + 8) % 4, (core + 2) % 2
    return ((x % 2) * 4 + z, y * 4 + (x // 2) * 2 + core)


def split3(value):
    high = value.astype(BF16).astype(F32)
    rest = value - high
    middle = rest.astype(BF16).astype(F32)
    return high, middle, rest - middle


def matmul(left, right):
    return lax.dot_general(left, right, (((1,), (0,)), ((), ())), preferred_element_type=F32)


def matmul_t(left, right):
    return lax.dot_general(left, right, (((1,), (1,)), ((), ())), preferred_element_type=F32)


def pick(index, values):
    out = values[-1]
    for i in range(len(values) - 2, -1, -1):
        out = jnp.where(index == i, values[i], out)
    return out


def kernel(
    pool_ref, label_ref, grad_pool_ref, grad_label_ref, objective_ref,
    rows_in, own, at, bt, za, km, acc_a, acc_b, part_a, part_b, first_in, second_in, sum_b, sum_b_in, t_own, ta, tb,
    w1a, w2a, wb, o1b, o2b, oa, ga, gb, g_in, stat_out, stat_in,
    ga_send, ga_recv, gb_send, gb_recv, pa_send, pa_recv, pb_send, pb_recv,
    ta_send, ta_recv, tb_send, tb_recv, ra_send, ra_recv, rb_send, rb_recv, st_send, st_recv, read_sem,
):
    width = pool_ref.shape[1]
    each = pool_ref.shape[0]
    both = 2 * each
    deep = width + 16
    na, nb = len(FIRST), len(SECOND)
    points = float(each * 128)
    x, y, z, core = place()

    def to_first(a):
        return device(x + a // 2, y, z, core + a % 2)

    def from_first(a):
        return device(x - a // 2, y, z, core + a % 2)

    def to_second(b):
        return device(x, y + pick(b, [v[0] for v in SECOND]), z + pick(b, [v[1] for v in SECOND]), core)

    def from_second(b):
        return device(x, y - pick(b, [v[0] for v in SECOND]), z - pick(b, [v[1] for v in SECOND]), core)

    def copy(src, dst, send, recv, target):
        return pltpu.make_async_remote_copy(
            src_ref=src, dst_ref=dst, send_sem=send, recv_sem=recv, device_id=target, device_id_type=MESH
        )

    first_others = [a for a in range(na) if a != OWN_FIRST]
    second_others = [b for b in range(nb) if b != OWN_SECOND]
    shared = range(2 * TWO_SIDED)

    def lanes(index, count=1):
        return pl.ds(pl.multiple_of(index * both * count, both * count), both * count)

    def block_lanes(index):
        return pl.ds(pl.multiple_of(index * both, both), both)

    def gather_first(a):
        return copy(own, at.at[:, block_lanes(a)], ga_send.at[a], ga_recv.at[a], from_first(a))

    def forward(a):
        return copy(
            at.at[:, block_lanes(a - 1)], at.at[:, block_lanes(a)], ga_send.at[a], ga_recv.at[a],
            device(x, y, z, core + 1),
        )

    def gather_second(b):
        if b in (0, 1):
            source = own
        else:
            at_neighbour = {2: 0, 3: jnp.where(core == 0, 0, 1), 4: 7, 5: 8, 7: 0, 8: 1, 9: jnp.where(core == 0, 8, 7)}[b]
            source = bt.at[pl.ds(0, width), block_lanes(at_neighbour)]
        first, other = RELAY[b]
        dy = jnp.where(core == 0, first[0], other[0])
        dz = jnp.where(core == 0, first[1], other[1])
        return copy(
            source, bt.at[pl.ds(0, width), block_lanes(b)], gb_send.at[b], gb_recv.at[b],
            device(x, y - dy, z - dz, core),
        )

    def partial_first(a):
        return copy(part_a, first_in.at[a], pa_send.at[a], pa_recv.at[a], from_first(a))

    def partial_second(b):
        return copy(part_b.at[:, block_lanes(b)], second_in.at[b], pb_send.at[b], pb_recv.at[b], to_second(b))

    def total_first(a):
        return copy(sum_b, sum_b_in.at[a], ta_send.at[a], ta_recv.at[a], from_first(a))

    def total_second(b):
        return copy(t_own, tb.at[:, block_lanes(b)], tb_send.at[b], tb_recv.at[b], from_second(b))

    def return_first(a):
        return copy(ga.at[:, block_lanes(a)], g_in.at[a], ra_send.at[a], ra_recv.at[a], to_first(a))

    def return_second(b):
        return copy(gb.at[:, block_lanes(b)], g_in.at[na + b], rb_send.at[b], rb_recv.at[b], to_second(b))

    def stats(slot):
        target = device(x, y - slot // 4, z - slot % 4, core)
        return copy(stat_out, stat_in.at[slot], st_send.at[slot], st_recv.at[slot], target)

    partners = [(0, 0, 0, 1), (1, 0, 0, 0), (3, 0, 0, 0), (2, 0, 0, 0)]
    partners += [(0, 1, 0, 0), (0, 3, 0, 0), (0, 0, 1, 0), (0, 0, 3, 0)]
    barrier = pltpu.get_barrier_semaphore()
    for dx, dy, dz, dk in partners:
        pl.semaphore_signal(
            barrier, inc=1, device_id=device(x + dx, y + dy, z + dz, core + dk), device_id_type=MESH
        )

    reads = [
        pltpu.make_async_copy(pool_ref, rows_in.at[pl.ds(0, each)], read_sem.at[0]),
        pltpu.make_async_copy(label_ref, rows_in.at[pl.ds(each, each)], read_sem.at[1]),
    ]
    for item in reads:
        item.start()
    sign = jnp.where(lax.broadcasted_iota(jnp.int32, (1, both), 1) < each, 1.0, -1.0).astype(F32)
    for item in reads:
        item.wait()
    rows = rows_in[...].astype(F32)
    block = rows.T.astype(BF16)
    own[...] = block
    at[:, pl.ds(OWN_FIRST * both, both)] = block
    bt[0:width, pl.ds(OWN_SECOND * both, both)] = block
    bt[deep:, :] = jnp.zeros((bt.shape[0] - deep, nb * both), BF16)
    acc_a[...] = jnp.zeros(acc_a.shape, F32)
    acc_b[...] = jnp.zeros(acc_b.shape, F32)

    pl.semaphore_wait(barrier, len(partners))

    for a in (2, 6, 1):
        gather_first(a).start()
    for b in (0, 1):
        gather_second(b).start()
    gather_first(4).start()

    place8 = lax.broadcasted_iota(jnp.int32, (8, both), 0)
    none8 = jnp.zeros((8, both), F32)
    ones8 = jnp.where(place8 < 3, 1.0, none8)
    sign8 = jnp.where(place8 == 0, sign, none8)

    def three_rows(parts, start):
        out = none8
        for i, part in enumerate(parts):
            out = jnp.where(place8 == start + i, part, out)
        return out

    def half_norms(value):
        return three_rows(split3(jnp.sum(value * value, axis=0, keepdims=True) * -0.5), 0)

    def take_first(a):
        here = block_lanes(a)
        value = at[:, here].astype(F32)
        za[here, 0:width] = value.T.astype(BF16)
        rest = jnp.concatenate([ones8, half_norms(value), jnp.zeros((width - 16, both), F32)], axis=0)
        za[here, width : 2 * width] = rest.T.astype(BF16)
        w1a[0:width, here] = (value * sign).astype(BF16)
        w1a[width:deep, here] = jnp.concatenate([sign8, none8], axis=0).astype(BF16)

    def take_second(b):
        here = block_lanes(b)
        value = bt[0:width, here].astype(F32)
        bt[width:deep, here] = jnp.concatenate([half_norms(value), ones8], axis=0).astype(BF16)
        wb[0:width, here] = (value * sign).astype(BF16)

    scale = math.log2(math.e) / width
    tile_sign = sign[:, 128:256]

    def sum_second(w, out):
        def body(pair, carry):
            here = lanes(pair, 2)
            out[:, here] = matmul(w[...], km[:, here])
            return carry

        lax.fori_loop(0, TWO_SIDED, body, 0)

    def turn(expected, following):
        for b in expected:
            gather_second(b).wait_recv()
        for b in following:
            gather_second(b).start()

    def once(t, steps, action):
        chosen = t == steps[0]
        for step in steps[1:]:
            chosen = chosen | (t == step)
        pl.when(chosen)(action)

    def form(pair, place, count):
        wide = lanes(pair, 2)
        here = lanes(place, 2 * count)
        product = matmul(za[here, :], bt[:, wide])
        value = jnp.exp2(product * scale)
        km[here, wide] = value.astype(BF16)
        tiles = [value[:, 128 * j : 128 * (j + 1)] for j in range(6)]
        across = (tiles[0] - tiles[2]) + (tiles[3] - tiles[5]) + (tiles[1] + tiles[4]) * tile_sign
        acc_a[here, :] += across
        parts = [
            jnp.sum(value[each * j : each * (j + 1)].reshape(each // 8, 8, 2 * both), axis=0) for j in range(4 * count)
        ]
        down = sum(parts[2::2], parts[0]) - sum(parts[3::2], parts[1])
        acc_b[:, lanes(jnp.minimum(pair, TWO_SIDED), 2)] += down

    def new_second(pair):
        take_second(2 * pair)
        take_second(2 * pair + 1)

    def second_done(pair):
        for b in (2 * pair, 2 * pair + 1):
            here = block_lanes(b)
            part_b[:, here] = jnp.sum(acc_b[:, here], axis=0, keepdims=True) * sign
            partial_second(b).start()

    def early_step(t, carry):
        pair = jnp.where(t < 6, t // 3, t - 6)
        ap = jnp.where(t < 6, pick(t % 3, (0, 1, 3)), 2)

        def relay_first(a):
            gather_first(a).wait_recv()
            forward(a + 1).start()

        once(t, (0,), lambda: turn((0, 1), (2, 3, 7, 8)))
        once(t, (3,), lambda: turn((2, 3, 7, 8), (4, 5, 9)))
        once(t, (0,), lambda: relay_first(2))
        once(t, (1,), lambda: relay_first(6))
        once(t, (4,), lambda: relay_first(4))

        def new_first():
            gather_first(2 * ap + 1).wait_recv()
            take_first(2 * ap)
            take_first(2 * ap + 1)

        once(t, (0, 3), lambda: new_second(pair))
        once(t, (0, 1, 2, 6), new_first)
        form(pair, ap, 1)
        once(t, (6, 7), lambda: second_done(pair))
        return carry

    def late_step(t, carry):
        pair = pick(t, (3, 2, 4))
        once(t, (1,), lambda: turn((4, 5), ()))
        once(t, (2,), lambda: turn((9,), ()))
        new_second(pair)
        form(pair, 0, 4)
        once(t, (1,), lambda: second_done(pair))
        return carry

    lax.fori_loop(0, 8, early_step, 0)
    lax.fori_loop(0, 3, late_step, 0)

    rows8 = none8
    for a in range(na):
        rows8 = jnp.where(place8 == a, jnp.sum(acc_a[a * both : (a + 1) * both, :].T, axis=0, keepdims=True), rows8)
    part_a[...] = rows8 * sign
    for a in first_others:
        partial_first(a).start()
    got = jnp.zeros((1, both), F32)
    for b in shared:
        partial_second(b).wait_recv()
        got = got + second_in[b]
    sum_b[...] = got
    for a in first_others:
        total_first(a).start()
    sum_second(w1a, o1b)

    def seen_from(value, a):
        dx, dk = FIRST[a]
        if dk:
            value = jnp.where(place8 % 2 == 0, pltpu.roll(value, 7, 0), pltpu.roll(value, 1, 0))
        return pltpu.roll(value, 2 * dx, 0) if dx else value

    total = part_a[...]
    for a in first_others:
        partial_first(a).wait_recv()
        total = total + seen_from(first_in[a], a)
    total = total + jnp.where(place8 == OWN_FIRST, got, 0.0)
    for a in first_others:
        total_first(a).wait_recv()
        total = total + jnp.where(place8 == a, sum_b_in[a], 0.0)
    total = total + pltpu.roll(total, each, 1)
    for a in range(na):
        ta[:, a * both : (a + 1) * both] = jnp.broadcast_to(total[a : a + 1], (8, both))
    mine = total[OWN_FIRST : OWN_FIRST + 1]
    t_own[...] = mine
    tb[:, pl.ds(OWN_SECOND * both, both)] = mine
    for b in (9, 4, 5, 8, 7, 3, 2, 1, 0):
        total_second(b).start()

    line = ta[0:1, :]
    local = jnp.sum(line, axis=1, keepdims=True) / (na * both)
    spread = 0.5 * jnp.sum(jnp.square(line - local), axis=1, keepdims=True)
    told = jnp.where(lax.broadcasted_iota(jnp.int32, (1, 128), 1) < 64, local, spread)
    stat_out[...] = told
    stat_in[0] = told
    for slot in range(1, 16):
        stats(slot).start()

    def weigh_first(a, carry):
        here = block_lanes(a)
        shifted = ta[0:1, here] - local
        w2a[0:width, here] = (w1a[0:width, here].astype(F32) * shifted).astype(BF16)
        w2a[width:deep, here] = jnp.concatenate([three_rows(split3(shifted * sign), 0), none8], axis=0).astype(BF16)
        return carry

    lax.fori_loop(0, na, weigh_first, 0)

    sum_second(w2a, o2b)
    for b in second_others:
        total_second(b).wait_recv()

    def weigh_second(b, carry):
        here = block_lanes(b)
        shifted = tb[0:1, here] - local
        wb[width : 2 * width, here] = (wb[0:width, here].astype(F32) * shifted).astype(BF16)
        tail = sign8 + three_rows(split3(shifted * sign), 1)
        wb[2 * width : 2 * width + 16, here] = jnp.concatenate([tail, none8], axis=0).astype(BF16)
        return carry

    lax.fori_loop(0, nb, weigh_second, 0)

    def first_sums(ap, carry):
        here = lanes(ap, 2)
        oa[:, here] = matmul_t(wb[...], km[here, :])
        return carry

    first_sums(2, 0)
    for slot in range(1, 16):
        stats(slot).wait_recv()
    every = stat_in[...]
    added = jnp.sum(every, axis=0)
    mean = added[0:1, 0:1] * (1.0 / 16.0)
    away = jnp.sum(jnp.square(every - mean), axis=0)
    spread = added[0:1, 64:65] + float(na * each) * away[0:1, 0:1]
    variance = 4.0 * spread / points**3 + 1e-08
    statistic = mean / points
    deviation = jnp.sqrt(variance)
    coef_a = 1.0 / (points * deviation)
    coef_b = -4.0 * statistic / (points**2 * (variance * deviation))
    objective_ref[...] = jnp.broadcast_to(statistic / deviation, objective_ref.shape)
    base = 2.0 * coef_a + 2.0 * coef_b * (local - mean)
    outer = sign * (-1.0 / width)

    def combine(value, shifted, plain, rho, weighted, tau):
        alpha = base + coef_b * shifted
        return (value * rho - plain) * (alpha * outer) + (value * tau - weighted) * (coef_b * outer)

    def gradient_first(a):
        here = block_lanes(a)
        low = 2 * width
        tau = oa[low + 1 : low + 2, here] + oa[low + 2 : low + 3, here] + oa[low + 3 : low + 4, here]
        return combine(
            at[:, here].astype(F32), ta[0:1, here] - local,
            oa[0:width, here], oa[low : low + 1, here], oa[width:low, here], tau,
        )

    def gradient_second(b):
        here = block_lanes(b)
        tau = o2b[width : width + 1, here] + o2b[width + 1 : width + 2, here] + o2b[width + 2 : width + 3, here]
        return combine(
            bt[0:width, here].astype(F32), tb[0:1, here] - local,
            o1b[0:width, here], o1b[width : width + 1, here], o2b[0:width, here], tau,
        )

    def finish_second(j, carry):
        b = 2 * TWO_SIDED - 1 - j
        gb[:, block_lanes(b)] = gradient_second(b).astype(BF16)
        return_second(b).start()
        return carry

    def finish_first(a):
        ga[:, block_lanes(a)] = gradient_first(a).astype(BF16)
        return_first(a).start()

    def finish_and_sum(j, carry):
        ap = pick(j, (2, 3, 1))
        finish_first(2 * ap)
        finish_first(2 * ap + 1)

        @pl.when(j == 0)
        def _():
            lax.fori_loop(0, 2 * TWO_SIDED, finish_second, 0)

        first_sums(pick(j, (3, 1, 0)), 0)
        return carry

    lax.fori_loop(0, 3, finish_and_sum, 0)
    finish_first(1)
    result = gradient_first(OWN_FIRST)
    for b in shared:
        return_second(b).wait_recv()
        result = result + g_in[na + b].astype(F32)
    for a in (1, 4, 5, 6, 7, 2, 3):
        return_first(a).wait_recv()
        result = result + g_in[a].astype(F32)
    result = result.T
    grad_pool_ref[...] = result[0:each]
    grad_label_ref[...] = result[each:both]

    for a in first_others:
        for item in (gather_first if a in (1, 2, 4, 6) else forward, partial_first, total_first, return_first):
            item(a).wait_send()
    for b in second_others:
        for item in (gather_second, total_second):
            item(b).wait_send()
    for b in shared:
        for item in (partial_second, return_second):
            item(b).wait_send()
    for slot in range(1, 16):
        stats(slot).wait_send()


def shards(pool, labeled):
    each, width = pool.shape
    both = 2 * each
    deep = width + 16
    na, nb = len(FIRST), len(SECOND)
    la, lb, ls = na * both, nb * both, 2 * TWO_SIDED * both
    dma = pltpu.SemaphoreType.DMA
    vmem = pl.BlockSpec(memory_space=pltpu.VMEM)
    scratch = [
        pltpu.VMEM((both, width), BF16),
        pltpu.VMEM((width, both), BF16),
        pltpu.VMEM((width, la), BF16),
        pltpu.VMEM((2 * width, lb), BF16),
        pltpu.VMEM((la, 2 * width), BF16),
        pltpu.VMEM((la, lb), BF16),
        pltpu.VMEM((la, 128), F32),
        pltpu.VMEM((8, ls + 2 * both), F32),
        pltpu.VMEM((8, both), F32),
        pltpu.VMEM((1, ls), F32),
        pltpu.VMEM((na, 8, both), F32),
        pltpu.VMEM((2 * TWO_SIDED, 1, both), F32),
        pltpu.VMEM((1, both), F32),
        pltpu.VMEM((na, 1, both), F32),
        pltpu.VMEM((1, both), F32),
        pltpu.VMEM((8, la), F32),
        pltpu.VMEM((1, lb), F32),
        pltpu.VMEM((deep, la), BF16),
        pltpu.VMEM((deep, la), BF16),
        pltpu.VMEM((width + deep, lb), BF16),
        pltpu.VMEM((deep, ls), F32),
        pltpu.VMEM((deep, ls), F32),
        pltpu.VMEM((width + deep, la), F32),
        pltpu.VMEM((width, la), BF16),
        pltpu.VMEM((width, ls), BF16),
        pltpu.VMEM((na + nb, width, both), BF16),
        pltpu.VMEM((1, 128), F32),
        pltpu.VMEM((16, 1, 128), F32),
    ]
    for _ in range(4):
        scratch += [dma((na,)), dma((na,)), dma((nb,)), dma((nb,))]
    scratch += [dma((16,)), dma((16,)), dma((2,))]
    grad_pool, grad_label, objective = pl.pallas_call(
        kernel,
        out_shape=(
            jax.ShapeDtypeStruct((each, width), F32),
            jax.ShapeDtypeStruct((each, width), F32),
            jax.ShapeDtypeStruct((8, 128), F32),
        ),
        in_specs=[pl.BlockSpec(memory_space=pl.ANY)] * 2,
        out_specs=(vmem, vmem, vmem),
        scratch_shapes=scratch,
        compiler_params=pltpu.CompilerParams(
            collective_id=0, has_side_effects=True, vmem_limit_bytes=60 * 2**20
        ),
    )(pool, labeled)

    def hand_on(pool_in, label_in, objective_in, pool_out, label_out, objective_out):
        pool_out[...] = pool_in[...]
        label_out[...] = label_in[...]
        objective_out[0, 0] = objective_in[0, 0]

    grad_pool, grad_label, objective = pl.pallas_call(
        hand_on,
        out_shape=(
            jax.ShapeDtypeStruct((each, width), F32),
            jax.ShapeDtypeStruct((each, width), F32),
            jax.ShapeDtypeStruct((1, 1), F32),
        ),
        in_specs=[vmem, vmem, vmem],
        out_specs=(vmem, vmem, pl.BlockSpec(memory_space=pltpu.SMEM)),
    )(grad_pool, grad_label, objective)
    return grad_pool, grad_label, objective.reshape(())


def solution(mesh):
    in_specs = (P(("row", "col"), None), P(("row", "col"), None))
    out_specs = (P(("row", "col"), None), P(("row", "col"), None), P())
    return jax.shard_map(shards, mesh=mesh, in_specs=in_specs, out_specs=out_specs, check_vma=False)
```

```python
import math

import jax
import jax.numpy as jnp
from jax import lax
from jax.experimental import pallas as pl
from jax.experimental.pallas import tpu as pltpu
from jax.sharding import PartitionSpec as P

MESH = pl.DeviceIdType.MESH
F32 = jnp.float32
BF16 = jnp.bfloat16

FIRST = tuple((dx, dk) for dx in range(4) for dk in range(2))
SECOND = ((0, 1), (-1, 0), (1, 1), (-1, 1), (1, 2), (2, -1), (0, 0), (0, 2), (2, 0), (2, 2))
OWN_FIRST = FIRST.index((0, 0))
OWN_SECOND = SECOND.index((0, 0))
RELAY = {
    0: ((0, 1), (0, 1)),
    1: ((-1, 0), (-1, 0)),
    2: ((1, 0), (1, 0)),
    3: ((-1, 0), (0, 1)),
    7: ((0, 1), (0, 1)),
    8: ((-1, 0), (-1, 0)),
    4: ((1, 0), (1, 0)),
    5: ((0, -1), (0, -1)),
    9: ((0, 2), (2, 0)),
}
TWO_SIDED = 3
SECOND_PAIRS = len(SECOND) // 2


def place():
    row, col = lax.axis_index("row"), lax.axis_index("col")
    return ((col // 2) % 2) * 2 + row // 4, col // 4, row % 4, col % 2


def device(x, y, z, core):
    x, y, z, core = (x + 8) % 4, (y + 8) % 4, (z + 8) % 4, (core + 2) % 2
    return ((x % 2) * 4 + z, y * 4 + (x // 2) * 2 + core)


def split3(value):
    high = value.astype(BF16).astype(F32)
    rest = value - high
    middle = rest.astype(BF16).astype(F32)
    return high, middle, rest - middle


def matmul(left, right):
    return lax.dot_general(left, right, (((1,), (0,)), ((), ())), preferred_element_type=F32)


def matmul_t(left, right):
    return lax.dot_general(left, right, (((1,), (1,)), ((), ())), preferred_element_type=F32)


def pick(index, values):
    out = values[-1]
    for i in range(len(values) - 2, -1, -1):
        out = jnp.where(index == i, values[i], out)
    return out


def kernel(
    pool_ref, label_ref, grad_pool_ref, grad_label_ref, objective_ref,
    rows_in, own, at, bt, za, km, acc_a, acc_b, part_a, part_b, first_in, second_in, sum_b, sum_b_in, t_own, ta, tb,
    w1a, w2a, wb, o1b, o2b, oa, ga, gb, g_in, stat_out, stat_in,
    ga_send, ga_recv, gb_send, gb_recv, pa_send, pa_recv, pb_send, pb_recv,
    ta_send, ta_recv, tb_send, tb_recv, ra_send, ra_recv, rb_send, rb_recv, st_send, st_recv, read_sem,
):
    width = pool_ref.shape[1]
    each = pool_ref.shape[0]
    both = 2 * each
    deep = width + 16
    na, nb = len(FIRST), len(SECOND)
    points = float(each * 128)
    x, y, z, core = place()

    def to_first(a):
        return device(x + a // 2, y, z, core + a % 2)

    def from_first(a):
        return device(x - a // 2, y, z, core + a % 2)

    def to_second(b):
        return device(x, y + pick(b, [v[0] for v in SECOND]), z + pick(b, [v[1] for v in SECOND]), core)

    def from_second(b):
        return device(x, y - pick(b, [v[0] for v in SECOND]), z - pick(b, [v[1] for v in SECOND]), core)

    def copy(src, dst, send, recv, target):
        return pltpu.make_async_remote_copy(
            src_ref=src, dst_ref=dst, send_sem=send, recv_sem=recv, device_id=target, device_id_type=MESH
        )

    first_others = [a for a in range(na) if a != OWN_FIRST]
    second_others = [b for b in range(nb) if b != OWN_SECOND]
    shared = range(2 * TWO_SIDED)

    def lanes(index, count=1):
        return pl.ds(pl.multiple_of(index * both * count, both * count), both * count)

    def block_lanes(index):
        return pl.ds(pl.multiple_of(index * both, both), both)

    def gather_first(a):
        return copy(own, at.at[:, block_lanes(a)], ga_send.at[a], ga_recv.at[a], from_first(a))

    def forward(a):
        return copy(
            at.at[:, block_lanes(a - 1)], at.at[:, block_lanes(a)], ga_send.at[a], ga_recv.at[a],
            device(x, y, z, core + 1),
        )

    def gather_second(b):
        if b in (0, 1):
            source = own
        else:
            at_neighbour = {2: 0, 3: jnp.where(core == 0, 0, 1), 4: 7, 5: 8, 7: 0, 8: 1, 9: jnp.where(core == 0, 8, 7)}[b]
            source = bt.at[pl.ds(0, width), block_lanes(at_neighbour)]
        first, other = RELAY[b]
        dy = jnp.where(core == 0, first[0], other[0])
        dz = jnp.where(core == 0, first[1], other[1])
        return copy(
            source, bt.at[pl.ds(0, width), block_lanes(b)], gb_send.at[b], gb_recv.at[b],
            device(x, y - dy, z - dz, core),
        )

    def partial_first(a):
        return copy(part_a, first_in.at[a], pa_send.at[a], pa_recv.at[a], from_first(a))

    def partial_second(b):
        return copy(part_b.at[:, block_lanes(b)], second_in.at[b], pb_send.at[b], pb_recv.at[b], to_second(b))

    def total_first(a):
        return copy(sum_b, sum_b_in.at[a], ta_send.at[a], ta_recv.at[a], from_first(a))

    def total_second(b):
        return copy(t_own, tb.at[:, block_lanes(b)], tb_send.at[b], tb_recv.at[b], from_second(b))

    def return_first(a):
        return copy(ga.at[:, block_lanes(a)], g_in.at[a], ra_send.at[a], ra_recv.at[a], to_first(a))

    def return_second(b):
        return copy(gb.at[:, block_lanes(b)], g_in.at[na + b], rb_send.at[b], rb_recv.at[b], to_second(b))

    def stats(slot):
        target = device(x, y - slot // 4, z - slot % 4, core)
        return copy(stat_out, stat_in.at[slot], st_send.at[slot], st_recv.at[slot], target)

    partners = [(0, 0, 0, 1), (1, 0, 0, 0), (3, 0, 0, 0), (2, 0, 0, 0)]
    partners += [(0, 1, 0, 0), (0, 3, 0, 0), (0, 0, 1, 0), (0, 0, 3, 0)]
    barrier = pltpu.get_barrier_semaphore()
    for dx, dy, dz, dk in partners:
        pl.semaphore_signal(
            barrier, inc=1, device_id=device(x + dx, y + dy, z + dz, core + dk), device_id_type=MESH
        )

    reads = [
        pltpu.make_async_copy(pool_ref, rows_in.at[pl.ds(0, each)], read_sem.at[0]),
        pltpu.make_async_copy(label_ref, rows_in.at[pl.ds(each, each)], read_sem.at[1]),
    ]
    for item in reads:
        item.start()
    sign = jnp.where(lax.broadcasted_iota(jnp.int32, (1, both), 1) < each, 1.0, -1.0).astype(F32)
    for item in reads:
        item.wait()
    rows = rows_in[...].astype(F32)
    block = rows.T.astype(BF16)
    own[...] = block
    at[:, pl.ds(OWN_FIRST * both, both)] = block
    bt[0:width, pl.ds(OWN_SECOND * both, both)] = block
    bt[deep:, :] = jnp.zeros((bt.shape[0] - deep, nb * both), BF16)
    acc_a[...] = jnp.zeros(acc_a.shape, F32)
    acc_b[...] = jnp.zeros(acc_b.shape, F32)

    pl.semaphore_wait(barrier, len(partners))

    for a in (2, 6, 1):
        gather_first(a).start()
    for b in (0, 1):
        gather_second(b).start()
    gather_first(4).start()

    place8 = lax.broadcasted_iota(jnp.int32, (8, both), 0)
    none8 = jnp.zeros((8, both), F32)
    ones8 = jnp.where(place8 < 3, 1.0, none8)
    sign8 = jnp.where(place8 == 0, sign, none8)

    def three_rows(parts, start):
        out = none8
        for i, part in enumerate(parts):
            out = jnp.where(place8 == start + i, part, out)
        return out

    def half_norms(value):
        return three_rows(split3(jnp.sum(value * value, axis=0, keepdims=True) * -0.5), 0)

    def take_first(a):
        here = block_lanes(a)
        value = at[:, here].astype(F32)
        za[here, 0:width] = value.T.astype(BF16)
        rest = jnp.concatenate([ones8, half_norms(value), jnp.zeros((width - 16, both), F32)], axis=0)
        za[here, width : 2 * width] = rest.T.astype(BF16)
        w1a[0:width, here] = (value * sign).astype(BF16)
        w1a[width:deep, here] = jnp.concatenate([sign8, none8], axis=0).astype(BF16)

    def take_second(b):
        here = block_lanes(b)
        value = bt[0:width, here].astype(F32)
        bt[width:deep, here] = jnp.concatenate([half_norms(value), ones8], axis=0).astype(BF16)
        wb[0:width, here] = (value * sign).astype(BF16)

    scale = math.log2(math.e) / width
    tile_sign = sign[:, 128:256]

    def sum_second(w, out):
        def body(pair, carry):
            here = lanes(pair, 2)
            out[:, here] = matmul(w[...], km[:, here])
            return carry

        lax.fori_loop(0, TWO_SIDED, body, 0)

    def turn(expected, following):
        for b in expected:
            gather_second(b).wait_recv()
        for b in following:
            gather_second(b).start()

    def once(t, steps, action):
        chosen = t == steps[0]
        for step in steps[1:]:
            chosen = chosen | (t == step)
        pl.when(chosen)(action)

    def form(pair, place, count):
        wide = lanes(pair, 2)
        here = lanes(place, 2 * count)
        product = matmul(za[here, :], bt[:, wide])
        value = jnp.exp2(product * scale)
        km[here, wide] = value.astype(BF16)
        tiles = [value[:, 128 * j : 128 * (j + 1)] for j in range(6)]
        across = (tiles[0] - tiles[2]) + (tiles[3] - tiles[5]) + (tiles[1] + tiles[4]) * tile_sign
        acc_a[here, :] += across
        parts = [
            jnp.sum(value[each * j : each * (j + 1)].reshape(each // 8, 8, 2 * both), axis=0) for j in range(4 * count)
        ]
        down = sum(parts[2::2], parts[0]) - sum(parts[3::2], parts[1])
        acc_b[:, lanes(jnp.minimum(pair, TWO_SIDED), 2)] += down

    def new_second(pair):
        take_second(2 * pair)
        take_second(2 * pair + 1)

    def second_done(pair):
        for b in (2 * pair, 2 * pair + 1):
            here = block_lanes(b)
            part_b[:, here] = jnp.sum(acc_b[:, here], axis=0, keepdims=True) * sign
            partial_second(b).start()

    def early_step(t, carry):
        ap = pick(t, (0, 1, 3, 2))

        def relay_first(a):
            gather_first(a).wait_recv()
            forward(a + 1).start()

        once(t, (0,), lambda: turn((0, 1), (2, 3, 7, 8)))
        once(t, (3,), lambda: turn((2, 3, 7, 8), (4, 5, 9)))
        once(t, (0,), lambda: relay_first(2))
        once(t, (1,), lambda: relay_first(6))
        once(t, (2,), lambda: relay_first(4))

        def new_first():
            gather_first(2 * ap + 1).wait_recv()
            take_first(2 * ap)
            take_first(2 * ap + 1)

        once(t, (0,), lambda: new_second(0))
        new_first()
        form(0, ap, 1)
        once(t, (3,), lambda: second_done(0))
        return carry

    def late_step(t, carry):
        pair = pick(t, (1, 3, 2, 4))
        once(t, (2,), lambda: turn((4, 5), ()))
        once(t, (3,), lambda: turn((9,), ()))
        new_second(pair)
        form(pair, 0, 4)
        once(t, (0, 2), lambda: second_done(pair))
        return carry

    lax.fori_loop(0, 4, early_step, 0)
    lax.fori_loop(0, 4, late_step, 0)

    rows8 = none8
    for a in range(na):
        rows8 = jnp.where(place8 == a, jnp.sum(acc_a[a * both : (a + 1) * both, :].T, axis=0, keepdims=True), rows8)
    part_a[...] = rows8 * sign
    for a in first_others:
        partial_first(a).start()
    got = jnp.zeros((1, both), F32)
    for b in shared:
        partial_second(b).wait_recv()
        got = got + second_in[b]
    sum_b[...] = got
    for a in first_others:
        total_first(a).start()
    sum_second(w1a, o1b)

    def seen_from(value, a):
        dx, dk = FIRST[a]
        if dk:
            value = jnp.where(place8 % 2 == 0, pltpu.roll(value, 7, 0), pltpu.roll(value, 1, 0))
        return pltpu.roll(value, 2 * dx, 0) if dx else value

    total = part_a[...]
    for a in first_others:
        partial_first(a).wait_recv()
        total = total + seen_from(first_in[a], a)
    total = total + jnp.where(place8 == OWN_FIRST, got, 0.0)
    for a in first_others:
        total_first(a).wait_recv()
        total = total + jnp.where(place8 == a, sum_b_in[a], 0.0)
    total = total + pltpu.roll(total, each, 1)
    for a in range(na):
        ta[:, a * both : (a + 1) * both] = jnp.broadcast_to(total[a : a + 1], (8, both))
    mine = total[OWN_FIRST : OWN_FIRST + 1]
    t_own[...] = mine
    tb[:, pl.ds(OWN_SECOND * both, both)] = mine
    for b in (9, 4, 5, 8, 7, 3, 2, 1, 0):
        total_second(b).start()

    line = ta[0:1, :]
    local = jnp.sum(line, axis=1, keepdims=True) / (na * both)
    spread = 0.5 * jnp.sum(jnp.square(line - local), axis=1, keepdims=True)
    told = jnp.where(lax.broadcasted_iota(jnp.int32, (1, 128), 1) < 64, local, spread)
    stat_out[...] = told
    stat_in[0] = told
    for slot in range(1, 16):
        stats(slot).start()

    def weigh_first(a, carry):
        here = block_lanes(a)
        shifted = ta[0:1, here] - local
        w2a[0:width, here] = (w1a[0:width, here].astype(F32) * shifted).astype(BF16)
        w2a[width:deep, here] = jnp.concatenate([three_rows(split3(shifted * sign), 0), none8], axis=0).astype(BF16)
        return carry

    lax.fori_loop(0, na, weigh_first, 0)

    sum_second(w2a, o2b)
    for b in second_others:
        total_second(b).wait_recv()

    def weigh_second(b, carry):
        here = block_lanes(b)
        shifted = tb[0:1, here] - local
        wb[width : 2 * width, here] = (wb[0:width, here].astype(F32) * shifted).astype(BF16)
        tail = sign8 + three_rows(split3(shifted * sign), 1)
        wb[2 * width : 2 * width + 16, here] = jnp.concatenate([tail, none8], axis=0).astype(BF16)
        return carry

    lax.fori_loop(0, nb, weigh_second, 0)

    def first_sums(ap, carry):
        here = lanes(ap, 2)
        oa[:, here] = matmul_t(wb[...], km[here, :])
        return carry

    first_sums(2, 0)
    for slot in range(1, 16):
        stats(slot).wait_recv()
    every = stat_in[...]
    added = jnp.sum(every, axis=0)
    mean = added[0:1, 0:1] * (1.0 / 16.0)
    away = jnp.sum(jnp.square(every - mean), axis=0)
    spread = added[0:1, 64:65] + float(na * each) * away[0:1, 0:1]
    variance = 4.0 * spread / points**3 + 1e-08
    statistic = mean / points
    deviation = jnp.sqrt(variance)
    coef_a = 1.0 / (points * deviation)
    coef_b = -4.0 * statistic / (points**2 * (variance * deviation))
    objective_ref[...] = jnp.broadcast_to(statistic / deviation, objective_ref.shape)
    base = 2.0 * coef_a + 2.0 * coef_b * (local - mean)
    outer = sign * (-1.0 / width)

    def combine(value, shifted, plain, rho, weighted, tau):
        alpha = base + coef_b * shifted
        return (value * rho - plain) * (alpha * outer) + (value * tau - weighted) * (coef_b * outer)

    def gradient_first(a):
        here = block_lanes(a)
        low = 2 * width
        tau = oa[low + 1 : low + 2, here] + oa[low + 2 : low + 3, here] + oa[low + 3 : low + 4, here]
        return combine(
            at[:, here].astype(F32), ta[0:1, here] - local,
            oa[0:width, here], oa[low : low + 1, here], oa[width:low, here], tau,
        )

    def gradient_second(b):
        here = block_lanes(b)
        tau = o2b[width : width + 1, here] + o2b[width + 1 : width + 2, here] + o2b[width + 2 : width + 3, here]
        return combine(
            bt[0:width, here].astype(F32), tb[0:1, here] - local,
            o1b[0:width, here], o1b[width : width + 1, here], o2b[0:width, here], tau,
        )

    def finish_second(j, carry):
        b = 2 * TWO_SIDED - 1 - j
        gb[:, block_lanes(b)] = gradient_second(b).astype(BF16)
        return_second(b).start()
        return carry

    def finish_first(a):
        ga[:, block_lanes(a)] = gradient_first(a).astype(BF16)
        return_first(a).start()

    def finish_and_sum(j, carry):
        ap = pick(j, (2, 3, 1))
        finish_first(2 * ap)
        finish_first(2 * ap + 1)

        @pl.when(j == 0)
        def _():
            lax.fori_loop(0, 2 * TWO_SIDED, finish_second, 0)

        first_sums(pick(j, (3, 1, 0)), 0)
        return carry

    lax.fori_loop(0, 3, finish_and_sum, 0)
    finish_first(1)
    result = gradient_first(OWN_FIRST)
    for b in shared:
        return_second(b).wait_recv()
        result = result + g_in[na + b].astype(F32)
    for a in (1, 4, 5, 6, 7, 2, 3):
        return_first(a).wait_recv()
        result = result + g_in[a].astype(F32)
    result = result.T
    grad_pool_ref[...] = result[0:each]
    grad_label_ref[...] = result[each:both]

    for a in first_others:
        for item in (gather_first if a in (1, 2, 4, 6) else forward, partial_first, total_first, return_first):
            item(a).wait_send()
    for b in second_others:
        for item in (gather_second, total_second):
            item(b).wait_send()
    for b in shared:
        for item in (partial_second, return_second):
            item(b).wait_send()
    for slot in range(1, 16):
        stats(slot).wait_send()


def shards(pool, labeled):
    each, width = pool.shape
    both = 2 * each
    deep = width + 16
    na, nb = len(FIRST), len(SECOND)
    la, lb, ls = na * both, nb * both, 2 * TWO_SIDED * both
    dma = pltpu.SemaphoreType.DMA
    vmem = pl.BlockSpec(memory_space=pltpu.VMEM)
    scratch = [
        pltpu.VMEM((both, width), BF16),
        pltpu.VMEM((width, both), BF16),
        pltpu.VMEM((width, la), BF16),
        pltpu.VMEM((2 * width, lb), BF16),
        pltpu.VMEM((la, 2 * width), BF16),
        pltpu.VMEM((la, lb), BF16),
        pltpu.VMEM((la, 128), F32),
        pltpu.VMEM((8, ls + 2 * both), F32),
        pltpu.VMEM((8, both), F32),
        pltpu.VMEM((1, ls), F32),
        pltpu.VMEM((na, 8, both), F32),
        pltpu.VMEM((2 * TWO_SIDED, 1, both), F32),
        pltpu.VMEM((1, both), F32),
        pltpu.VMEM((na, 1, both), F32),
        pltpu.VMEM((1, both), F32),
        pltpu.VMEM((8, la), F32),
        pltpu.VMEM((1, lb), F32),
        pltpu.VMEM((deep, la), BF16),
        pltpu.VMEM((deep, la), BF16),
        pltpu.VMEM((width + deep, lb), BF16),
        pltpu.VMEM((deep, ls), F32),
        pltpu.VMEM((deep, ls), F32),
        pltpu.VMEM((width + deep, la), F32),
        pltpu.VMEM((width, la), BF16),
        pltpu.VMEM((width, ls), BF16),
        pltpu.VMEM((na + nb, width, both), BF16),
        pltpu.VMEM((1, 128), F32),
        pltpu.VMEM((16, 1, 128), F32),
    ]
    for _ in range(4):
        scratch += [dma((na,)), dma((na,)), dma((nb,)), dma((nb,))]
    scratch += [dma((16,)), dma((16,)), dma((2,))]
    grad_pool, grad_label, objective = pl.pallas_call(
        kernel,
        out_shape=(
            jax.ShapeDtypeStruct((each, width), F32),
            jax.ShapeDtypeStruct((each, width), F32),
            jax.ShapeDtypeStruct((8, 128), F32),
        ),
        in_specs=[pl.BlockSpec(memory_space=pl.ANY)] * 2,
        out_specs=(vmem, vmem, vmem),
        scratch_shapes=scratch,
        compiler_params=pltpu.CompilerParams(
            collective_id=0, has_side_effects=True, vmem_limit_bytes=60 * 2**20
        ),
    )(pool, labeled)

    def hand_on(pool_in, label_in, objective_in, pool_out, label_out, objective_out):
        pool_out[...] = pool_in[...]
        label_out[...] = label_in[...]
        objective_out[0, 0] = objective_in[0, 0]

    grad_pool, grad_label, objective = pl.pallas_call(
        hand_on,
        out_shape=(
            jax.ShapeDtypeStruct((each, width), F32),
            jax.ShapeDtypeStruct((each, width), F32),
            jax.ShapeDtypeStruct((1, 1), F32),
        ),
        in_specs=[vmem, vmem, vmem],
        out_specs=(vmem, vmem, pl.BlockSpec(memory_space=pltpu.SMEM)),
    )(grad_pool, grad_label, objective)
    return grad_pool, grad_label, objective.reshape(())


def solution(mesh):
    in_specs = (P(("row", "col"), None), P(("row", "col"), None))
    out_specs = (P(("row", "col"), None), P(("row", "col"), None), P())
    return jax.shard_map(shards, mesh=mesh, in_specs=in_specs, out_specs=out_specs, check_vma=False)
```
